256 devices in a mesh: member: 16 (over z, core), space: 16 (over y, x).
Axes of the slice: x: 4, y: 4, z: 8, core: 2. Of those that a mesh axis runs over, the one named last changes fastest.
Arguments:
- collective_model_vectors: float32 [48, 16, 128, 512], P('member', None, 'space'), may hold values from -8 to 8
- obs_columns: int32 [128, 16, 64], P('space'), may hold values from 0 to 31
- obs_values: float32 [128, 16, 64], P('space'), may hold values from -6 to 6
- obs_precision: float32 [128, 16, 64], P('space'), may hold values from 0.5 to 8
- obs_mask: int32 [128, 16, 64], P('space'), may hold values 0 or 1
- obs_counts: int32 [128, 16], P('space'), may hold values from 16 to 64
Outputs:
- analysis: float32 [48, 16, 128, 512], P('member', None, 'space')
The draws below stay inside these ranges and needn't reach their ends.
Inputs may be any that keep to these rules, and one draw needn't show every extreme that they name: Slots from obs_counts on are ignored.
All inputs are finite; a program needn't handle non-finite values. No bound on the sum of `obs_mask` on one device may be relied on, other than what follows from the above.
Results may differ from the reference program's by a relative error of at most 0.0003.
Values sent between devices are 32-bit elements; how exact they have to be, the bound alone decides.
A program may use at most 192 MiB of HBM per device.

```python
import math
import jax
import jax.numpy as jnp
from jax import lax

LEV = 16
CX = 8
BW = 32
OBS = 64
MG_LEVELS = 3
COARSE_SWEEPS = 3
VCYCLES = 2
ENS = 48
NX = 128
NY = 512
N_MEMBER = 16


def draw_collective_model_vectors(key, part):
    key = jax.random.fold_in(key, 7)
    key_list = jax.random.split(key, 6)
    mode_count = 4
    row_frac = jnp.arange(NX, dtype=jnp.float32)[:, None] / NX
    col_frac = jnp.arange(NY, dtype=jnp.float32)[None, :] / NY
    row_waves = jax.random.randint(key_list[0], (ENS, 1, mode_count), 1, 4).astype(jnp.float32)
    col_waves = jax.random.randint(key_list[1], (ENS, 1, mode_count), 1, 4).astype(jnp.float32)
    phases = jax.random.uniform(key_list[2], (ENS, LEV, mode_count), jnp.float32, -math.pi, math.pi)
    amplitudes = jnp.clip(0.6 * jax.random.normal(key_list[3], (ENS, LEV, mode_count), jnp.float32), -1.5, 1.5)
    rough_part = jnp.clip(0.3 * jax.random.normal(key_list[5], (ENS, LEV, NX, NY), jnp.float32), -1.8, 1.8)
    result_field = rough_part
    for wave_index in range(mode_count):
        row_term = row_waves[:, :, wave_index, None, None] * row_frac
        col_term = col_waves[:, :, wave_index, None, None] * col_frac
        phase_arg = 2.0 * math.pi * (row_term + col_term) + phases[:, :, wave_index, None, None]
        result_field = result_field + amplitudes[:, :, wave_index, None, None] * jnp.cos(phase_arg)
    return result_field


def with_ends(values, key, least, high):
    extent = values.shape
    place = [jax.random.randint(jax.random.fold_in(key, axis), (), 0, extent[axis]) for axis in range(len(extent))]
    values = values.at[tuple(place)].set(least)
    longest = extent.index(max(extent))
    place[longest] = (place[longest] + 1) % extent[longest]
    return values.at[tuple(place)].set(high)


def steps_of(own_key, extent, pieces, low, high):
    loudness = 1.0
    for axis_at, blocks in pieces:
        draws = jax.random.uniform(jax.random.fold_in(jax.random.fold_in(own_key, 6), axis_at), (blocks,), jnp.float32, low / len(pieces), high / len(pieces))
        loudness = loudness * jnp.repeat(jnp.exp(draws), extent[axis_at] // blocks).reshape((-1,) + (1,) * (len(extent) - 1 - axis_at))
    return loudness


def bell_draw(rng, shape, deviation, bound, pieces=(), kind=jnp.bfloat16):
    drawn = deviation * jax.random.normal(rng, shape, jnp.float32)
    if pieces:
        drawn = drawn * steps_of(rng, shape, pieces, -0.22, 0.18)
    return jnp.clip(drawn, -bound, bound).astype(kind)


def setup_inputs(seed: int = 0) -> dict:
    arg_keys = jax.random.split(jax.random.key(seed), 7)
    return {
        "collective_model_vectors": draw_collective_model_vectors(jax.random.fold_in(arg_keys[6], 71), 0),
        "obs_columns": with_ends(jax.random.randint(arg_keys[1], (NX, N_MEMBER, OBS), 0, BW), jax.random.fold_in(arg_keys[1], 1), 0, BW - 1).astype(jnp.int32),
        "obs_values": bell_draw(arg_keys[2], (NX, N_MEMBER, OBS), 1.0, 6.0, ((0, 16),), jnp.float32),
        "obs_precision": jnp.clip(jnp.exp(math.log(8.0) - 2.7725887 * jax.random.uniform(arg_keys[3], (NX, N_MEMBER, OBS), jnp.float32) ** steps_of(arg_keys[3], (NX, N_MEMBER, OBS), ((0, 16),), -0.2, 0.2)), 0.5, 8.0),
        "obs_mask": with_ends((jax.random.randint(arg_keys[4], (NX, N_MEMBER, OBS), 0, 4) < 3).astype(jnp.int32), jax.random.fold_in(arg_keys[4], 1), 0, 1),
        "obs_counts": with_ends(jax.random.randint(arg_keys[5], (NX, N_MEMBER), OBS // 4, OBS + 1), jax.random.fold_in(arg_keys[5], 1), OBS // 4, OBS).astype(jnp.int32),
    }


diffusion_rate = 0.2
vertical_rate = 0.2
helmholtz_shift = 0.001
stress_link_multiplier = 0.04
highest = lax.Precision.HIGHEST

def helmholtz_whole(grid_field, spacing):
    padded = jnp.pad(grid_field, ((0, 0), (0, 0), (1, 1), (1, 1)))
    neighbours = padded[:, :, 2:, 1:-1] + padded[:, :, :-2, 1:-1]
    neighbours = neighbours + padded[:, :, 1:-1, 2:] + padded[:, :, 1:-1, :-2]
    return helmholtz_shift * grid_field + (4.0 * grid_field - neighbours) / (spacing * spacing)

def restrict(grid_field):
    lead, vertical_layers_number, rows, cols = grid_field.shape
    return grid_field.reshape(lead, vertical_layers_number, rows // 2, 2, cols // 2, 2).mean(axis=(3, 5))

def prolong(grid_field):
    return jnp.repeat(jnp.repeat(grid_field, 2, axis=2), 2, axis=3)

def vcycle(stress_distribution, source, grid_level):
    spacing = 2.0 ** grid_level
    diagonal = helmholtz_shift + 8.0 / (spacing * spacing)
    if grid_level == MG_LEVELS:
        solved = source / diagonal
        for sweep_index in range(COARSE_SWEEPS - 1):
            solved = solved + (source - helmholtz_whole(solved, spacing)) / diagonal
        return solved
    if stress_distribution is None:
        stress_distribution = source / diagonal
    else:
        stress_distribution = stress_distribution + (source - helmholtz_whole(stress_distribution, spacing)) / diagonal
    residual_field = source - helmholtz_whole(stress_distribution, spacing)
    correction = vcycle(None, restrict(residual_field), grid_level + 1)
    stress_distribution = stress_distribution + prolong(correction)
    return stress_distribution + (source - helmholtz_whole(stress_distribution, spacing)) / diagonal

def predict_sample(lone_sample_vector):
    state = lone_sample_vector[None]
    padded = jnp.pad(state, ((0, 0), (0, 0), (1, 1), (1, 1)))
    neighbours = padded[:, :, 2:, 1:-1] + padded[:, :, :-2, 1:-1]
    neighbours = neighbours + padded[:, :, 1:-1, 2:] + padded[:, :, 1:-1, :-2]
    above = jnp.concatenate([state[:, 1:], state[:, -1:]], axis=1)
    below = jnp.concatenate([state[:, :1], state[:, :-1]], axis=1)
    propagated_later = state + diffusion_rate * (neighbours - 4.0 * state) + vertical_rate * (above + below - 2.0 * state)
    stress_distribution = vcycle(None, propagated_later, 0)
    for cycle_index in range(1, VCYCLES):
        stress_distribution = vcycle(stress_distribution, propagated_later, 0)
    return (propagated_later - stress_link_multiplier * stress_distribution)[0]

def factor_inverse(system):
    members = system.shape[0]
    order_index = lax.broadcasted_iota(jnp.int32, (members, 1, 1), 0)

    def factor_step(column_index, lower):
        column_index = jnp.asarray(column_index).astype(jnp.int32)
        lower_row = lax.dynamic_slice_in_dim(lower, column_index, 1, 0)[0]
        column = lax.dynamic_slice_in_dim(system, column_index, 1, 1)[:, 0]
        column = column - jnp.einsum('ikxb,kxb->ixb', lower, lower_row, precision=highest)
        pivot = jnp.sqrt(lax.dynamic_slice_in_dim(column, column_index, 1, 0))
        fresh = jnp.where(order_index >= column_index, column / pivot, jnp.zeros_like(column))
        return lax.dynamic_update_slice_in_dim(lower, fresh[:, None], column_index, 1)
    lower = lax.fori_loop(0, members, factor_step, jnp.zeros_like(system))

    def inverse_step(row_index, inverse):
        row_index = jnp.asarray(row_index).astype(jnp.int32)
        lower_row = lax.dynamic_slice_in_dim(lower, row_index, 1, 0)[0]
        pivot = lax.dynamic_slice_in_dim(lower_row, row_index, 1, 0)
        carried = jnp.einsum('kxb,kfxb->fxb', lower_row, inverse, precision=highest)
        unit = (order_index == row_index).astype(system.dtype)
        fresh = (unit - carried) / pivot
        return lax.dynamic_update_slice_in_dim(inverse, fresh[None], row_index, 0)
    return lax.fori_loop(0, members, inverse_step, jnp.zeros_like(system))

def ensemble_weights(predicted, obs_values, obs_precision, obs_mask, obs_counts):
    members = predicted.shape[0]
    obs_mean = lax.optimization_barrier(jnp.mean(predicted, axis=0))
    spread = predicted - obs_mean
    innovation = obs_values - obs_mean
    valid_obs = (lax.broadcasted_iota(jnp.int32, obs_values.shape, 2) < obs_counts[:, :, None]).astype(predicted.dtype)
    weight = valid_obs * obs_mask.astype(predicted.dtype) * obs_precision
    weighted_spread = spread * weight[None]
    identity = jnp.eye(members, dtype=predicted.dtype)
    system = (members - 1.0) * identity[:, :, None, None] + jnp.einsum('exbo,fxbo->efxb', weighted_spread, spread, precision=highest)
    target = jnp.einsum('exbo,xbo->exb', weighted_spread, innovation, precision=highest)
    inverse = factor_inverse(system)
    middle = jnp.einsum('efxb,fxb->exb', inverse, target, precision=highest)
    mean_weights = jnp.einsum('fexb,fxb->xbe', inverse, middle, precision=highest)
    square_root = math.sqrt(members - 1.0) * jnp.einsum('kjxb->xbjk', inverse)
    return mean_weights[..., :, None] + square_root

def analyse_rows(row_inputs):
    row_state, columns, values, precision_rows, mask_rows, counts_rows = row_inputs
    members, vertical_layers_number, strip_rows, mesh_breadth = row_state.shape
    blocks = columns.shape[1]
    block_width = mesh_breadth // blocks
    state5 = row_state.reshape(members, vertical_layers_number, strip_rows, blocks, block_width)
    column_mean = lax.optimization_barrier(jnp.mean(state5, axis=1))
    selector = (columns[:, :, :, None] == lax.broadcasted_iota(jnp.int32, (1, 1, 1, block_width), 3)).astype(row_state.dtype)
    predicted = jnp.einsum('exbw,xbow->exbo', column_mean, selector, precision=highest)
    transform = ensemble_weights(predicted, values, precision_rows, mask_rows, counts_rows)
    state_mean = lax.optimization_barrier(jnp.mean(state5, axis=0))
    perturb = state5 - state_mean
    analysed = state_mean + jnp.einsum('jlxbw,xbjk->klxbw', perturb, transform, precision=highest)
    return analysed.reshape(members, vertical_layers_number, strip_rows, mesh_breadth)

def reference(collective_model_vectors, obs_columns, obs_values, obs_precision, obs_mask, obs_counts):
    predicted_output = lax.map(predict_sample, collective_model_vectors)
    members, vertical_layers_number, grid_rows, mesh_breadth = predicted_output.shape
    strips = grid_rows // CX
    strip_major = jnp.moveaxis(predicted_output.reshape(members, vertical_layers_number, strips, CX, mesh_breadth), 2, 0)
    blocks = obs_columns.shape[1]
    obs_shape = (strips, CX, blocks, obs_columns.shape[2])
    analysed = lax.map(analyse_rows, (strip_major, obs_columns.reshape(obs_shape), obs_values.reshape(obs_shape), obs_precision.reshape(obs_shape), obs_mask.reshape(obs_shape), obs_counts.reshape(strips, CX, blocks)))
    return jnp.moveaxis(analysed, 0, 2).reshape(members, vertical_layers_number, grid_rows, mesh_breadth)
```

```python
import functools
import math

import jax
import jax.numpy as jnp
from jax import lax
from jax.experimental import pallas as pl
from jax.experimental.pallas import tpu as pltpu
from jax.sharding import PartitionSpec as P

LEV, CX, BW, OBS, ENS, NX, NY = 16, 8, 32, 64, 48, 128, 512
GROUP = 16
PER = ENS // GROUP
HALF = NY // 2
BLOCKS = HALF // BW
SHIFT = 0.001
MESH = pl.DeviceIdType.MESH
f32, bf16 = jnp.float32, jnp.bfloat16


def split3(x):
    a = x.astype(bf16)
    r = x - a.astype(f32)
    b = r.astype(bf16)
    c = (r - b.astype(f32)).astype(bf16)
    return a, b, c


def dot(a, b):
    return jnp.dot(a, b, preferred_element_type=f32)


def exact_dot(x, selector):
    a, b, c = split3(x)
    return dot(a, selector) + (dot(b, selector) + dot(c, selector))


def iota2(shape, dim):
    return lax.broadcasted_iota(jnp.int32, shape, dim)


def lane_right(x, n):
    return jnp.where(iota2(x.shape, 1) < n, 0.0, pltpu.roll(x, n, 1))


def lane_left(x, n):
    return jnp.where(iota2(x.shape, 1) >= x.shape[1] - n, 0.0, pltpu.roll(x, x.shape[1] - n, 1))


def strip_down(x):
    return jnp.where(iota2(x.shape, 0) < 1, 0.0, pltpu.roll(x, 1, 0))


def strip_up(x):
    return jnp.where(iota2(x.shape, 0) >= x.shape[0] - 1, 0.0, pltpu.roll(x, x.shape[0] - 1, 0))


def each_phase(op, row):
    return jnp.stack([op(row[c]) for c in range(row.shape[0])], axis=0)


def neighbours(rows, width):
    count = len(rows)
    above = [each_phase(strip_down, rows[-1])] + rows[:-1]
    below = rows[1:] + [each_phase(strip_up, rows[0])]
    out = []
    for k in range(count):
        row = rows[k]
        phases = row.shape[0]
        first = lane_right(row[phases - 1], width)[None]
        last = lane_left(row[0], width)[None]
        if phases == 1:
            side = first + last
        else:
            side = jnp.concatenate([first, row[:-1]], axis=0) + jnp.concatenate([row[1:], last], axis=0)
        out.append((above[k] + below[k]) + side)
    return out


def smooth(p, f, level, width=1):
    h2 = 4.0**level
    d = SHIFT + 8.0 / h2
    a = 1.0 - (SHIFT + 4.0 / h2) / d
    n = neighbours(p, width)
    return [a * x + (1.0 / d) * y + (1.0 / (h2 * d)) * z for x, y, z in zip(p, f, n)]


def residual(p, f, level):
    h2 = 4.0**level
    n = neighbours(p, 1)
    return [y - (SHIFT + 4.0 / h2) * x + (1.0 / h2) * z for x, y, z in zip(p, f, n)]


def restrict(rows):
    out = []
    for k in range(len(rows) // 2):
        t = rows[2 * k] + rows[2 * k + 1]
        phases = t.shape[0]
        if phases == 1:
            even = (iota2(t[0].shape, 1) & 1) == 0
            other = jnp.where(even, pltpu.roll(t[0], 127, 1), pltpu.roll(t[0], 1, 1))
            out.append(0.25 * (t + other[None]))
        else:
            out.append(jnp.stack([0.25 * (t[2 * c] + t[2 * c + 1]) for c in range(phases // 2)], axis=0))
    return out


def add_prolonged(p, coarse):
    out = []
    for k in range(len(p)):
        c = coarse[k // 2]
        if c.shape[0] < p[k].shape[0]:
            c = jnp.stack([c[i // 2] for i in range(p[k].shape[0])], axis=0)
        out.append(p[k] + c)
    return out


def vcycle(p, f, level):
    d = SHIFT + 8.0 / 4.0**level
    if level == 3:
        p = [x * (1.0 / d) for x in f]
        for _ in range(2):
            p = smooth(p, f, 3, 2)
        return p
    if p is None:
        p = [x * (1.0 / d) for x in f]
    else:
        p = smooth(p, f, level)
    r = residual(p, f, level)
    c = vcycle(None, restrict(r), level + 1)
    p = add_prolonged(p, c)
    return smooth(p, f, level)


def plane_forecast(f):
    p = vcycle(None, f, 0)
    p = vcycle(p, f, 0)
    return [x - 0.04 * y for x, y in zip(f, p)]


def send_all(axis, src, dst, send_sem, recv_sem):
    me = lax.axis_index(axis)

    @pl.loop(1, GROUP)
    def _(i):
        to = lax.rem(me + i, GROUP)
        pltpu.make_async_remote_copy(
            src.at[to], dst.at[me], send_sem, recv_sem, device_id={axis: to}, device_id_type=MESH
        ).start()

    pltpu.make_async_copy(src.at[me], dst.at[me], recv_sem).start()


def arrived(dst, recv_sem):
    pltpu.make_async_copy(dst, dst, recv_sem).wait()


def sent(src, send_sem):
    part = src.at[pl.ds(0, GROUP - 1)]
    pltpu.make_async_copy(part, part, send_sem).wait()


def partial_advance(qv, pm, wsend, esend):
    for lev in range(LEV):
        x = qv[pm, lev]
        near = qv[pm, min(lev + 1, LEV - 1)] + qv[pm, max(lev - 1, 0)]
        side = lane_right(x, 1) + lane_left(x, 1)
        wsend[pm, lev] = 0.2 * ((near + side) + (strip_down(x) + strip_up(x))) - 0.2 * x


def multigrid(pm, wrecv, erecv, perm, permt, work, fsend):
    plane = exact_dot(wrecv[pm].reshape(NX, NY), perm[...])
    for c in range(4):
        work[c] = plane[:, 128 * c : 128 * (c + 1)]
    top = exact_dot(erecv[:, 2 * pm, :], perm[...])
    bottom = exact_dot(erecv[:, 2 * pm + 1, :], perm[...])
    rows = []
    for rp in range(CX):
        x = [work[c, pl.ds(rp, GROUP, stride=CX), :] for c in range(4)]
        if rp == 0:
            x = [x[c] + 0.2 * strip_down(bottom[:, 128 * c : 128 * (c + 1)]) for c in range(4)]
        if rp == CX - 1:
            x = [x[c] + 0.2 * strip_up(top[:, 128 * c : 128 * (c + 1)]) for c in range(4)]
        rows.append(jnp.stack(x, axis=0))
    done = plane_forecast(rows)
    for rp in range(CX):
        for c in range(4):
            work[c, pl.ds(rp, GROUP, stride=CX), :] = done[rp][c]
    plane = jnp.concatenate([work[c] for c in range(4)], axis=1)
    fsend[pm] = exact_dot(plane, permt[...]).reshape(GROUP, CX, NY)


def to_rows(pm, frecv, flat, zsend):
    for c in range(4):
        flat[c] = frecv[pm, :, :, 128 * c : 128 * (c + 1)].reshape(LEV * CX, 128)
    for row in range(CX):
        for c in range(4):
            at = 128 * (c % 2)
            zsend[pm, 2 * row + c // 2, :, at : at + 128] = flat[c, pl.ds(row, LEV, stride=CX), :]


def observation_sums(cols, vals, precs, masks, counts, row, half):
    first = pl.multiple_of(half * BLOCKS, BLOCKS)
    col = cols[row, pl.ds(first, BLOCKS), :]
    val = vals[row, pl.ds(first, BLOCKS), :]
    prec = precs[row, pl.ds(first, BLOCKS), :]
    mask = masks[row, pl.ds(first, BLOCKS), :].astype(f32)
    row_counts = counts[pl.ds(row, 1), :].astype(f32)
    lane = iota2((BLOCKS, 2 * BLOCKS), 1)
    mine = lane == iota2((BLOCKS, 2 * BLOCKS), 0) + half * BLOCKS
    count = jnp.sum(jnp.where(mine, jnp.broadcast_to(row_counts, mine.shape), 0.0), axis=1, keepdims=True)
    slot = iota2((BLOCKS, OBS), 1).astype(f32)
    weight = jnp.where(slot < count, mask * prec, 0.0)
    value = weight * val
    place = iota2((BLOCKS, HALF), 1)
    within = place & (BW - 1)
    wsum = jnp.zeros((BLOCKS, HALF), f32)
    vsum = jnp.zeros((BLOCKS, HALF), f32)
    for o in range(OBS):
        hit = within == col[:, o : o + 1]
        wsum = wsum + jnp.where(hit, weight[:, o : o + 1], 0.0)
        vsum = vsum + jnp.where(hit, value[:, o : o + 1], 0.0)
    own = (place >> 5) == iota2((BLOCKS, HALF), 0)
    return jnp.where(own, wsum, 0.0), jnp.where(own, vsum, 0.0)


def analyse(zrecv, wsum, vsum, cm, lhs, call, expand, emat, asend):
    for j in range(ENS):
        x = zrecv[j % PER, j // PER]
        cm[j : j + 1, :] = jnp.sum(x, axis=0, keepdims=True) * (1.0 / LEV)
    means = cm[...]
    pbar = jnp.mean(means, axis=0, keepdims=True)
    spread = means - pbar
    cm[...] = spread
    for j in range(ENS):
        lhs[8 * j : 8 * (j + 1), :] = wsum * cm[j : j + 1, :]
    lhs[8 * ENS : 8 * ENS + 8, :] = vsum - wsum * pbar
    system = lax.dot_general(
        lhs[...], spread, (((1,), (1,)), ((), ())), precision=lax.Precision.HIGHEST, preferred_element_type=f32
    )
    lane = iota2((BLOCKS, 128), 1)
    pad = jnp.zeros((BLOCKS, 128 - ENS), f32)
    u = []
    for i in range(ENS):
        s = jnp.concatenate([system[8 * i : 8 * (i + 1), :], pad], axis=1)
        u.append(s + jnp.where(lane == i, ENS - 1.0, 0.0) + jnp.where(lane == i + 64, 1.0, 0.0))
    target = jnp.concatenate([system[8 * ENS : 8 * ENS + 8, :], pad], axis=1)
    for k in range(ENS):
        inv = 1.0 / u[k][:, k : k + 1]
        r = u[k] * inv
        for i in range(k + 1, ENS):
            u[i] = u[i] - u[k][:, i : i + 1] * r
    weights = jnp.zeros((BLOCKS, 128), f32)
    for k in range(ENS):
        scale = lax.rsqrt(u[k][:, k : k + 1])
        row = jnp.where(lane < ENS, pltpu.roll(u[k], 64, 1), 0.0) * scale
        weights = weights + row * jnp.sum(row * target, axis=1, keepdims=True)
        call[8 * k : 8 * (k + 1), :] = row * math.sqrt(ENS - 1.0)
    call[8 * ENS : 8 * ENS + 8, :] = weights
    call[8 * ENS + 8 :, :] = jnp.zeros((120, 128), f32)
    group = iota2((ENS, 128), 1) >> 3
    for g in range(4):
        t = jnp.transpose(call[128 * g : 128 * (g + 1), :])[:ENS]
        for k in range(16 if g < 3 else 1):
            emat[16 * g + k] = exact_dot(jnp.where(group == k, t, 0.0), expand[...])
    xbar = zrecv[0, 0]
    for j in range(1, ENS):
        xbar = xbar + zrecv[j % PER, j // PER]
    xbar = xbar * (1.0 / ENS)

    def mean_step(j, base):
        x = zrecv[lax.rem(j, PER), j // PER] - xbar
        zrecv[lax.rem(j, PER), j // PER] = x
        return base + x * emat[ENS, pl.ds(j, 1), :]

    base = lax.fori_loop(0, ENS, mean_step, xbar)
    step = PER
    for k in range(0, ENS, step):

        def apply(j, acc, k=k):
            x = zrecv[lax.rem(j, PER), j // PER]
            return tuple(acc[n] + x * emat[k + n, pl.ds(j, 1), :] for n in range(step))

        acc = lax.fori_loop(0, k + step, apply, (base,) * step)
        for n in range(step):
            asend[k // PER, n] = acc[n]


def kernel(q, cols, vals, precs, masks, counts, out, qv, wsend, wrecv, esend, erecv, perm, permt, work, fsend,
           frecv, flat, zsend, zrecv, cm, lhs, call, expand, emat, asend, arecv, qsem, ssem, rsem):
    load = pltpu.make_async_copy(q, qv, qsem)
    load.start()
    barrier = pltpu.get_barrier_semaphore()
    for axis in ("space", "member"):
        me = lax.axis_index(axis)

        @pl.loop(1, GROUP)
        def _(i, axis=axis, me=me):
            pl.semaphore_signal(barrier, inc=1, device_id={axis: lax.rem(me + i, GROUP)}, device_id_type=MESH)

    src = iota2((NY, NY), 0)
    dst = iota2((NY, NY), 1)
    perm[...] = (dst == ((src & 3) << 7) + (src >> 2)).astype(f32).astype(bf16)
    permt[...] = (src == ((dst & 3) << 7) + (dst >> 2)).astype(f32).astype(bf16)
    expand[...] = ((iota2((128, HALF), 0) & 7) == (iota2((128, HALF), 1) >> 5)).astype(f32).astype(bf16)
    load.wait()
    for pm in range(PER):
        for lev in range(LEV):
            esend[lev, 2 * pm : 2 * pm + 1, :] = qv[pm, lev, 0:1, :]
            esend[lev, 2 * pm + 1 : 2 * pm + 2, :] = qv[pm, lev, CX - 1 : CX, :]
    partial_advance(qv, 0, wsend, esend)
    pl.semaphore_wait(barrier, 2 * (GROUP - 1))
    send_all("space", esend, erecv, ssem.at[0], rsem.at[0])
    send_all("space", wsend.at[0], wrecv.at[0], ssem.at[1], rsem.at[1])
    for pm in range(1, PER):
        partial_advance(qv, pm, wsend, esend)
        send_all("space", wsend.at[pm], wrecv.at[pm], ssem.at[1 + pm], rsem.at[1 + pm])

    member = lax.axis_index("member")
    wsum, vsum = observation_sums(cols, vals, precs, masks, counts, member // 2, lax.rem(member, 2))

    def forward(pm):
        arrived(frecv.at[pm], rsem.at[4 + pm])
        to_rows(pm, frecv, flat, zsend)
        send_all("member", zsend.at[pm], zrecv.at[pm], ssem.at[7 + pm], rsem.at[7 + pm])

    arrived(erecv, rsem.at[0])
    for pm in range(PER):
        arrived(wrecv.at[pm], rsem.at[1 + pm])
        multigrid(pm, wrecv, erecv, perm, permt, work, fsend)
        send_all("space", fsend.at[pm], frecv.at[pm], ssem.at[4 + pm], rsem.at[4 + pm])
        if pm:
            forward(pm - 1)
    forward(PER - 1)
    for pm in range(PER):
        arrived(zrecv.at[pm], rsem.at[7 + pm])
    analyse(zrecv, wsum, vsum, cm, lhs, call, expand, emat, asend)
    send_all("member", asend, arecv, ssem.at[10], rsem.at[10])
    sent(esend, ssem.at[0])
    for pm in range(PER):
        sent(wsend.at[pm], ssem.at[1 + pm])
        sent(fsend.at[pm], ssem.at[4 + pm])
        sent(zsend.at[pm], ssem.at[7 + pm])
    arrived(arecv, rsem.at[10])
    for pm in range(PER):
        for m in range(GROUP):
            for c in range(2):
                at = 128 * c
                flat[2 * (m % 2) + c, pl.ds(m // 2, LEV, stride=CX), :] = arecv[m, pm, :, at : at + 128]
        for c in range(4):
            out[pm, :, 128 * c : 128 * (c + 1)] = flat[c]
    sent(asend, ssem.at[10])


def local(q, cols, vals, precs, masks, counts):
    vmem = pl.BlockSpec(memory_space=pltpu.VMEM)
    strips = pltpu.VMEM((PER, LEV, CX, NY), f32)
    rows = pltpu.VMEM((PER, GROUP, LEV, HALF), f32)
    edges = pltpu.VMEM((LEV, 2 * PER, NY), f32)
    back = pltpu.VMEM((GROUP, PER, LEV, HALF), f32)
    out = pl.pallas_call(
        kernel,
        out_shape=jax.ShapeDtypeStruct((PER, LEV * CX, NY), f32),
        in_specs=[pl.BlockSpec(memory_space=pl.ANY)] + [vmem] * 5,
        out_specs=vmem,
        scratch_shapes=[
            strips, strips, strips, edges, edges,
            pltpu.VMEM((NY, NY), bf16), pltpu.VMEM((NY, NY), bf16), pltpu.VMEM((4, NX, 128), f32),
            strips, strips, pltpu.VMEM((4, LEV * CX, 128), f32), rows, rows,
            pltpu.VMEM((ENS, HALF), f32), pltpu.VMEM((8 * ENS + 8, HALF), f32), pltpu.VMEM((512, 128), f32),
            pltpu.VMEM((128, HALF), bf16), pltpu.VMEM((ENS + 1, ENS, HALF), f32), back, back,
            pltpu.SemaphoreType.DMA, pltpu.SemaphoreType.DMA((11,)), pltpu.SemaphoreType.DMA((11,)),
        ],
        compiler_params=pltpu.CompilerParams(
            collective_id=0, has_side_effects=True, vmem_limit_bytes=40 * 1024 * 1024
        ),
        name="forecast_analysis",
    )(q, cols, vals, precs, masks, counts)
    return out.reshape(PER, LEV, CX, NY)


def solution(mesh):
    return jax.shard_map(
        local,
        mesh=mesh,
        in_specs=(
            P("member", None, "space", None),
            P("space", None, None),
            P("space", None, None),
            P("space", None, None),
            P("space", None, None),
            P("space", None),
        ),
        out_specs=P("member", None, "space", None),
        check_vma=False,
    )
```

```python
import functools
import math

import jax
import jax.numpy as jnp
from jax import lax
from jax.experimental import pallas as pl
from jax.experimental.pallas import tpu as pltpu
from jax.sharding import PartitionSpec as P

LEV, CX, BW, OBS, ENS, NX, NY = 16, 8, 32, 64, 48, 128, 512
GROUP = 16
PER = ENS // GROUP
HALF = NY // 2
BLOCKS = HALF // BW
SHIFT = 0.001
MESH = pl.DeviceIdType.MESH
f32, bf16 = jnp.float32, jnp.bfloat16


def split3(x):
    a = x.astype(bf16)
    r = x - a.astype(f32)
    b = r.astype(bf16)
    c = (r - b.astype(f32)).astype(bf16)
    return a, b, c


def dot(a, b):
    return jnp.dot(a, b, preferred_element_type=f32)


def exact_dot(x, selector):
    a, b, c = split3(x)
    return dot(a, selector) + (dot(b, selector) + dot(c, selector))


def iota2(shape, dim):
    return lax.broadcasted_iota(jnp.int32, shape, dim)


def lane_right(x, n):
    return jnp.where(iota2(x.shape, 1) < n, 0.0, pltpu.roll(x, n, 1))


def lane_left(x, n):
    return jnp.where(iota2(x.shape, 1) >= x.shape[1] - n, 0.0, pltpu.roll(x, x.shape[1] - n, 1))


def strip_down(x):
    return jnp.where(iota2(x.shape, 0) < 1, 0.0, pltpu.roll(x, 1, 0))


def strip_up(x):
    return jnp.where(iota2(x.shape, 0) >= x.shape[0] - 1, 0.0, pltpu.roll(x, x.shape[0] - 1, 0))


def each_phase(op, row):
    return jnp.stack([op(row[c]) for c in range(row.shape[0])], axis=0)


def neighbours(rows, width):
    count = len(rows)
    above = [each_phase(strip_down, rows[-1])] + rows[:-1]
    below = rows[1:] + [each_phase(strip_up, rows[0])]
    out = []
    for k in range(count):
        row = rows[k]
        phases = row.shape[0]
        first = lane_right(row[phases - 1], width)[None]
        last = lane_left(row[0], width)[None]
        if phases == 1:
            side = first + last
        else:
            side = jnp.concatenate([first, row[:-1]], axis=0) + jnp.concatenate([row[1:], last], axis=0)
        out.append((above[k] + below[k]) + side)
    return out


def smooth(p, f, level, width=1):
    h2 = 4.0**level
    d = SHIFT + 8.0 / h2
    a = 1.0 - (SHIFT + 4.0 / h2) / d
    n = neighbours(p, width)
    return [a * x + (1.0 / d) * y + (1.0 / (h2 * d)) * z for x, y, z in zip(p, f, n)]


def residual(p, f, level):
    h2 = 4.0**level
    n = neighbours(p, 1)
    return [y - (SHIFT + 4.0 / h2) * x + (1.0 / h2) * z for x, y, z in zip(p, f, n)]


def restrict(rows):
    out = []
    for k in range(len(rows) // 2):
        t = rows[2 * k] + rows[2 * k + 1]
        phases = t.shape[0]
        if phases == 1:
            even = (iota2(t[0].shape, 1) & 1) == 0
            other = jnp.where(even, pltpu.roll(t[0], 127, 1), pltpu.roll(t[0], 1, 1))
            out.append(0.25 * (t + other[None]))
        else:
            out.append(jnp.stack([0.25 * (t[2 * c] + t[2 * c + 1]) for c in range(phases // 2)], axis=0))
    return out


def add_prolonged(p, coarse):
    out = []
    for k in range(len(p)):
        c = coarse[k // 2]
        if c.shape[0] < p[k].shape[0]:
            c = jnp.stack([c[i // 2] for i in range(p[k].shape[0])], axis=0)
        out.append(p[k] + c)
    return out


def vcycle(p, f, level):
    d = SHIFT + 8.0 / 4.0**level
    if level == 3:
        p = [x * (1.0 / d) for x in f]
        for _ in range(2):
            p = smooth(p, f, 3, 2)
        return p
    if p is None:
        p = [x * (1.0 / d) for x in f]
    else:
        p = smooth(p, f, level)
    r = residual(p, f, level)
    c = vcycle(None, restrict(r), level + 1)
    p = add_prolonged(p, c)
    return smooth(p, f, level)


def plane_forecast(f):
    p = vcycle(None, f, 0)
    p = vcycle(p, f, 0)
    return [x - 0.04 * y for x, y in zip(f, p)]


def send_all(axis, src, dst, send_sem, recv_sem):
    me = lax.axis_index(axis)

    @pl.loop(1, GROUP)
    def _(i):
        to = lax.rem(me + i, GROUP)
        pltpu.make_async_remote_copy(
            src.at[to], dst.at[me], send_sem, recv_sem, device_id={axis: to}, device_id_type=MESH
        ).start()

    pltpu.make_async_copy(src.at[me], dst.at[me], recv_sem).start()


def arrived(dst, recv_sem):
    pltpu.make_async_copy(dst, dst, recv_sem).wait()


def sent(src, send_sem):
    part = src.at[pl.ds(0, GROUP - 1)]
    pltpu.make_async_copy(part, part, send_sem).wait()


def partial_advance(qv, pm, wsend):
    for lev in range(LEV):
        x = qv[pm, lev]
        near = qv[pm, min(lev + 1, LEV - 1)] + qv[pm, max(lev - 1, 0)]
        side = lane_right(x, 1) + lane_left(x, 1)
        wsend[pm, lev] = 0.2 * ((near + side) + (strip_down(x) + strip_up(x))) - 0.2 * x


def multigrid(pm, wrecv, erecv, perm, permt, work, fsend):
    plane = exact_dot(wrecv[pm].reshape(NX, NY), perm[...])
    for c in range(4):
        work[c] = plane[:, 128 * c : 128 * (c + 1)]
    top = exact_dot(erecv[pm, :, 0, :], perm[...])
    bottom = exact_dot(erecv[pm, :, 1, :], perm[...])
    rows = []
    for rp in range(CX):
        x = [work[c, pl.ds(rp, GROUP, stride=CX), :] for c in range(4)]
        if rp == 0:
            x = [x[c] + 0.2 * strip_down(bottom[:, 128 * c : 128 * (c + 1)]) for c in range(4)]
        if rp == CX - 1:
            x = [x[c] + 0.2 * strip_up(top[:, 128 * c : 128 * (c + 1)]) for c in range(4)]
        rows.append(jnp.stack(x, axis=0))
    done = plane_forecast(rows)
    for rp in range(CX):
        for c in range(4):
            work[c, pl.ds(rp, GROUP, stride=CX), :] = done[rp][c]
    plane = jnp.concatenate([work[c] for c in range(4)], axis=1)
    fsend[pm] = exact_dot(plane, permt[...]).reshape(GROUP, CX, NY)


def column_means(pm, frecv, csend):
    total = frecv[pm, 0]
    for lev in range(1, LEV):
        total = total + frecv[pm, lev]
    total = total * (1.0 / LEV)
    for row in range(CX):
        for half in range(2):
            csend[2 * row + half, pm : pm + 1, :] = total[row : row + 1, half * HALF : (half + 1) * HALF]


def to_rows(pm, frecv, flat, zsend):
    for c in range(4):
        flat[c] = frecv[pm, :, :, 128 * c : 128 * (c + 1)].reshape(LEV * CX, 128)
    for row in range(CX):
        for c in range(4):
            at = 128 * (c % 2)
            zsend[pm, 2 * row + c // 2, :, at : at + 128] = flat[c, pl.ds(row, LEV, stride=CX), :]


def observation_sums(cols, vals, precs, masks, counts, row, half):
    first = pl.multiple_of(half * BLOCKS, BLOCKS)
    col = cols[row, pl.ds(first, BLOCKS), :]
    val = vals[row, pl.ds(first, BLOCKS), :]
    prec = precs[row, pl.ds(first, BLOCKS), :]
    mask = masks[row, pl.ds(first, BLOCKS), :].astype(f32)
    row_counts = counts[pl.ds(row, 1), :].astype(f32)
    lane = iota2((BLOCKS, 2 * BLOCKS), 1)
    mine = lane == iota2((BLOCKS, 2 * BLOCKS), 0) + half * BLOCKS
    count = jnp.sum(jnp.where(mine, jnp.broadcast_to(row_counts, mine.shape), 0.0), axis=1, keepdims=True)
    slot = iota2((BLOCKS, OBS), 1).astype(f32)
    weight = jnp.where(slot < count, mask * prec, 0.0)
    value = weight * val
    place = iota2((BLOCKS, HALF), 1)
    within = place & (BW - 1)
    wsum = jnp.zeros((BLOCKS, HALF), f32)
    vsum = jnp.zeros((BLOCKS, HALF), f32)
    for o in range(OBS):
        hit = within == col[:, o : o + 1]
        wsum = wsum + jnp.where(hit, weight[:, o : o + 1], 0.0)
        vsum = vsum + jnp.where(hit, value[:, o : o + 1], 0.0)
    own = (place >> 5) == iota2((BLOCKS, HALF), 0)
    return jnp.where(own, wsum, 0.0), jnp.where(own, vsum, 0.0)


def make_transform(crecv, wsum, vsum, cm, lhs, call, expand, emat):
    for m in range(GROUP):
        cm[PER * m : PER * (m + 1), :] = crecv[m]
    means = cm[...]
    pbar = jnp.mean(means, axis=0, keepdims=True)
    spread = means - pbar
    cm[...] = spread
    for j in range(ENS):
        lhs[8 * j : 8 * (j + 1), :] = wsum * cm[j : j + 1, :]
    lhs[8 * ENS : 8 * ENS + 8, :] = vsum - wsum * pbar
    system = lax.dot_general(
        lhs[...], spread, (((1,), (1,)), ((), ())), precision=lax.Precision.HIGHEST, preferred_element_type=f32
    )
    lane = iota2((BLOCKS, 128), 1)
    pad = jnp.zeros((BLOCKS, 128 - ENS), f32)
    u = []
    for i in range(ENS):
        s = jnp.concatenate([system[8 * i : 8 * (i + 1), :], pad], axis=1)
        u.append(s + jnp.where(lane == i, ENS - 1.0, 0.0) + jnp.where(lane == i + 64, 1.0, 0.0))
    target = jnp.concatenate([system[8 * ENS : 8 * ENS + 8, :], pad], axis=1)
    for k in range(ENS):
        inv = 1.0 / u[k][:, k : k + 1]
        r = u[k] * inv
        for i in range(k + 1, ENS):
            u[i] = u[i] - u[k][:, i : i + 1] * r
    weights = jnp.zeros((BLOCKS, 128), f32)
    for k in range(ENS):
        scale = lax.rsqrt(u[k][:, k : k + 1])
        row = jnp.where(lane < ENS, pltpu.roll(u[k], 64, 1), 0.0) * scale
        weights = weights + row * jnp.sum(row * target, axis=1, keepdims=True)
        call[8 * k : 8 * (k + 1), :] = row * math.sqrt(ENS - 1.0)
    call[8 * ENS : 8 * ENS + 8, :] = weights
    call[8 * ENS + 8 :, :] = jnp.zeros((120, 128), f32)
    for g in range(4):
        count, depth = (16, 16 * (g + 1)) if g < 3 else (1, ENS)
        t = jnp.transpose(call[128 * g : 128 * (g + 1), :])[:depth]
        group = iota2((depth, 128), 1) >> 3
        high = t.astype(bf16).astype(f32)
        low = t - high
        parts = []
        for k in range(count):
            mine = group == k
            both = jnp.concatenate([jnp.where(mine, high, 0.0), jnp.where(mine, low, 0.0)], axis=1)
            parts.append(both.astype(bf16))
        wide = dot(jnp.concatenate(parts, axis=0), expand[...])
        for k in range(count):
            emat[16 * g + k, 0:depth, :] = wide[depth * k : depth * (k + 1), :]


def member_sum(zrecv, pm, total):
    for m in range(GROUP):
        total = zrecv[pm, m] if total is None else total + zrecv[pm, m]
    return total


def apply_transform(zrecv, total, emat, asend, arecv, send_sem, recv_sem):
    xbar = total * (1.0 / ENS)

    def mean_step(m, base):
        for pm in range(PER):
            x = zrecv[pm, m] - xbar
            zrecv[pm, m] = x
            base = base + x * emat[ENS, pl.ds(PER * m + pm, 1), :]
        return base

    base = lax.fori_loop(0, GROUP, mean_step, xbar)
    me = lax.axis_index("member")

    def one_target(to):
        def step(m, acc):
            acc = list(acc)
            for pm in range(PER):
                x = zrecv[pm, m]
                for n in range(PER):
                    acc[n] = acc[n] + x * emat[PER * to + n, pl.ds(PER * m + pm, 1), :]
            return tuple(acc)

        acc = lax.fori_loop(0, to, step, (base,) * PER)
        for n in range(PER):
            total = acc[n]
            for pm in range(n + 1):
                total = total + zrecv[pm, to] * emat[PER * to + n, pl.ds(PER * to + pm, 1), :]
            asend[to, n] = total

    @pl.loop(1, GROUP)
    def _(i):
        to = lax.rem(me + i, GROUP)
        one_target(to)
        pltpu.make_async_remote_copy(
            asend.at[to], arecv.at[me], send_sem, recv_sem.at[me], device_id={"member": to}, device_id_type=MESH
        ).start()

    one_target(me)
    pltpu.make_async_copy(asend.at[me], arecv.at[me], recv_sem.at[me]).start()


def kernel(q, cols_in, vals_in, precs_in, masks_in, counts_in, out, qv, cols, vals, precs, masks, counts, wsend, wrecv,
           esend, erecv, perm, permt, work, fsend, frecv, flat, zsend, zrecv, csend, crecv, cm, lhs, call, expand, emat,
           asend, arecv, strips, lsem, ssem, rsem, asem):
    given = ((q, qv), (cols_in, cols), (vals_in, vals), (precs_in, precs), (masks_in, masks), (counts_in, counts))
    loads = [pltpu.make_async_copy(a, b, lsem.at[n]) for n, (a, b) in enumerate(given)]
    for load in loads:
        load.start()
    barrier = pltpu.get_barrier_semaphore()
    for axis in ("member", "space"):
        me = lax.axis_index(axis)
        for i in (8, 7, 9, 6, 10, 5, 11, 4, 12, 3, 13, 2, 14, 1, 15):
            pl.semaphore_signal(barrier, inc=1, device_id={axis: lax.rem(me + i, GROUP)}, device_id_type=MESH)

    src = iota2((NY, NY), 0)
    dst = iota2((NY, NY), 1)
    perm[...] = (dst == ((src & 3) << 7) + (src >> 2)).astype(f32).astype(bf16)
    permt[...] = (src == ((dst & 3) << 7) + (dst >> 2)).astype(f32).astype(bf16)
    expand[...] = ((iota2((256, HALF), 0) & 7) == (iota2((256, HALF), 1) >> 5)).astype(f32).astype(bf16)
    loads[0].wait()
    for pm in range(PER):
        for lev in range(LEV):
            esend[pm, lev, 0:1, :] = qv[pm, lev, 0:1, :]
            esend[pm, lev, 1:2, :] = qv[pm, lev, CX - 1 : CX, :]
        partial_advance(qv, pm, wsend)
    for load in loads[1:]:
        load.wait()
    member = lax.axis_index("member")
    wsum, vsum = observation_sums(cols, vals, precs, masks, counts, member // 2, lax.rem(member, 2))
    pl.semaphore_wait(barrier, 2 * (GROUP - 1))

    def to_planes(pm):
        send_all("space", esend.at[pm], erecv.at[pm], ssem.at[pm], rsem.at[pm])
        send_all("space", wsend.at[pm], wrecv.at[pm], ssem.at[3 + pm], rsem.at[3 + pm])

    def solve(pm):
        arrived(erecv.at[pm], rsem.at[pm])
        arrived(wrecv.at[pm], rsem.at[3 + pm])
        multigrid(pm, wrecv, erecv, perm, permt, work, fsend)
        send_all("space", fsend.at[pm], frecv.at[pm], ssem.at[6 + pm], rsem.at[6 + pm])

    def to_blocks(pm):
        arrived(frecv.at[pm], rsem.at[6 + pm])
        column_means(pm, frecv, csend)
        if pm == PER - 1:
            send_all("member", csend, crecv, ssem.at[12], rsem.at[12])
        to_rows(pm, frecv, flat, zsend)
        send_all("member", zsend.at[pm], zrecv.at[pm], ssem.at[9 + pm], rsem.at[9 + pm])

    to_planes(0)
    to_planes(1)
    solve(0)
    to_planes(2)
    solve(1)
    to_blocks(0)
    solve(2)
    to_blocks(1)
    to_blocks(2)
    arrived(zrecv.at[0], rsem.at[9])
    total = member_sum(zrecv, 0, None)
    arrived(crecv, rsem.at[12])
    make_transform(crecv, wsum, vsum, cm, lhs, call, expand, emat)
    arrived(zrecv.at[1], rsem.at[10])
    total = member_sum(zrecv, 1, total)
    arrived(zrecv.at[2], rsem.at[11])
    total = member_sum(zrecv, 2, total)
    apply_transform(zrecv, total, emat, asend, arecv, ssem.at[13], asem)
    for pm in range(PER):
        sent(esend.at[pm], ssem.at[pm])
        sent(wsend.at[pm], ssem.at[3 + pm])
        sent(fsend.at[pm], ssem.at[6 + pm])
        sent(zsend.at[pm], ssem.at[9 + pm])
    sent(csend, ssem.at[12])

    @pl.loop(0, GROUP)
    def _(i):
        m = lax.rem(member + GROUP - i, GROUP)
        arrived(arecv.at[m], asem.at[m])
        for pm in range(PER):
            for c in range(2):
                strips[pm, 2 * lax.rem(m, 2) + c, pl.ds(m // 2, LEV, stride=CX), :] = arecv[m, pm, :, 128 * c : 128 * (c + 1)]

    for pm in range(PER):
        for c in range(4):
            out[pm, :, 128 * c : 128 * (c + 1)] = strips[pm, c]
    sent(asend, ssem.at[13])


def local(q, cols, vals, precs, masks, counts):
    hbm = pl.BlockSpec(memory_space=pl.ANY)
    strips = pltpu.VMEM((PER, LEV, CX, NY), f32)
    rows = pltpu.VMEM((PER, GROUP, LEV, HALF), f32)
    edges = pltpu.VMEM((PER, LEV, 2, NY), f32)
    back = pltpu.VMEM((GROUP, PER, LEV, HALF), f32)
    means = pltpu.VMEM((GROUP, PER, HALF), f32)
    slots = (CX, GROUP, OBS)
    dma = pltpu.SemaphoreType.DMA
    out = pl.pallas_call(
        kernel,
        out_shape=jax.ShapeDtypeStruct((PER, LEV * CX, NY), f32),
        in_specs=[hbm] * 6,
        out_specs=pl.BlockSpec(memory_space=pltpu.VMEM),
        scratch_shapes=[
            strips, pltpu.VMEM(slots, jnp.int32), pltpu.VMEM(slots, f32), pltpu.VMEM(slots, f32),
            pltpu.VMEM(slots, jnp.int32), pltpu.VMEM((CX, GROUP), jnp.int32), strips, strips, edges, edges,
            pltpu.VMEM((NY, NY), bf16), pltpu.VMEM((NY, NY), bf16), pltpu.VMEM((4, NX, 128), f32),
            strips, strips, pltpu.VMEM((4, LEV * CX, 128), f32), rows, rows, means, means,
            pltpu.VMEM((ENS, HALF), f32), pltpu.VMEM((8 * ENS + 8, HALF), f32), pltpu.VMEM((512, 128), f32),
            pltpu.VMEM((256, HALF), bf16), pltpu.VMEM((ENS + 1, ENS, HALF), f32), back, back,
            pltpu.VMEM((PER, 4, LEV * CX, 128), f32), dma((6,)), dma((14,)), dma((13,)), dma((GROUP,)),
        ],
        compiler_params=pltpu.CompilerParams(
            collective_id=0, has_side_effects=True, vmem_limit_bytes=56 * 1024 * 1024
        ),
        name="forecast_analysis",
    )(q, cols, vals, precs, masks, counts)
    return out.reshape(PER, LEV, CX, NY)


def solution(mesh):
    return jax.shard_map(
        local,
        mesh=mesh,
        in_specs=(
            P("member", None, "space", None),
            P("space", None, None),
            P("space", None, None),
            P("space", None, None),
            P("space", None, None),
            P("space", None),
        ),
        out_specs=P("member", None, "space", None),
        check_vma=False,
    )
```

```python
import functools
import math

import jax
import jax.numpy as jnp
from jax import lax
from jax.experimental import pallas as pl
from jax.experimental.pallas import tpu as pltpu
from jax.sharding import PartitionSpec as P

LEV, CX, BW, OBS, ENS, NX, NY = 16, 8, 32, 64, 48, 128, 512
GROUP = 16
PER = ENS // GROUP
HALF = NY // 2
BLOCKS = HALF // BW
SHIFT = 0.001
MESH = pl.DeviceIdType.MESH
f32, bf16 = jnp.float32, jnp.bfloat16


def split3(x):
    a = x.astype(bf16)
    r = x - a.astype(f32)
    b = r.astype(bf16)
    c = (r - b.astype(f32)).astype(bf16)
    return a, b, c


def dot(a, b):
    return jnp.dot(a, b, preferred_element_type=f32)


def exact_dot(x, selector):
    a, b, c = split3(x)
    return dot(a, selector) + (dot(b, selector) + dot(c, selector))


def iota2(shape, dim):
    return lax.broadcasted_iota(jnp.int32, shape, dim)


def lane_right(x, n):
    return jnp.where(iota2(x.shape, 1) < n, 0.0, pltpu.roll(x, n, 1))


def lane_left(x, n):
    return jnp.where(iota2(x.shape, 1) >= x.shape[1] - n, 0.0, pltpu.roll(x, x.shape[1] - n, 1))


def strip_down(x):
    return jnp.where(iota2(x.shape, 0) < 1, 0.0, pltpu.roll(x, 1, 0))


def strip_up(x):
    return jnp.where(iota2(x.shape, 0) >= x.shape[0] - 1, 0.0, pltpu.roll(x, x.shape[0] - 1, 0))


def each_phase(op, row):
    return jnp.stack([op(row[c]) for c in range(row.shape[0])], axis=0)


def neighbours(rows, width):
    count = len(rows)
    above = [each_phase(strip_down, rows[-1])] + rows[:-1]
    below = rows[1:] + [each_phase(strip_up, rows[0])]
    out = []
    for k in range(count):
        row = rows[k]
        phases = row.shape[0]
        first = lane_right(row[phases - 1], width)[None]
        last = lane_left(row[0], width)[None]
        if phases == 1:
            side = first + last
        else:
            side = jnp.concatenate([first, row[:-1]], axis=0) + jnp.concatenate([row[1:], last], axis=0)
        out.append((above[k] + below[k]) + side)
    return out


def smooth(p, f, level, width=1):
    h2 = 4.0**level
    d = SHIFT + 8.0 / h2
    a = 1.0 - (SHIFT + 4.0 / h2) / d
    n = neighbours(p, width)
    return [a * x + (1.0 / d) * y + (1.0 / (h2 * d)) * z for x, y, z in zip(p, f, n)]


def residual(p, f, level):
    h2 = 4.0**level
    n = neighbours(p, 1)
    return [y - (SHIFT + 4.0 / h2) * x + (1.0 / h2) * z for x, y, z in zip(p, f, n)]


def restrict(rows):
    out = []
    for k in range(len(rows) // 2):
        t = rows[2 * k] + rows[2 * k + 1]
        phases = t.shape[0]
        if phases == 1:
            even = (iota2(t[0].shape, 1) & 1) == 0
            other = jnp.where(even, pltpu.roll(t[0], 127, 1), pltpu.roll(t[0], 1, 1))
            out.append(0.25 * (t + other[None]))
        else:
            out.append(jnp.stack([0.25 * (t[2 * c] + t[2 * c + 1]) for c in range(phases // 2)], axis=0))
    return out


def add_prolonged(p, coarse):
    out = []
    for k in range(len(p)):
        c = coarse[k // 2]
        if c.shape[0] < p[k].shape[0]:
            c = jnp.stack([c[i // 2] for i in range(p[k].shape[0])], axis=0)
        out.append(p[k] + c)
    return out


def vcycle(p, f, level):
    d = SHIFT + 8.0 / 4.0**level
    if level == 3:
        p = [x * (1.0 / d) for x in f]
        for _ in range(2):
            p = smooth(p, f, 3, 2)
        return p
    if p is None:
        p = [x * (1.0 / d) for x in f]
    else:
        p = smooth(p, f, level)
    r = residual(p, f, level)
    c = vcycle(None, restrict(r), level + 1)
    p = add_prolonged(p, c)
    return smooth(p, f, level)


def plane_forecast(f):
    p = vcycle(None, f, 0)
    p = vcycle(p, f, 0)
    return [x - 0.04 * y for x, y in zip(f, p)]


def far_first(n):
    half = n // 2
    return GROUP // 2 + (2 * (n % 2) - 1) * half


def send_all(axis, src, dst, send_sem, recv_sem):
    me = lax.axis_index(axis)

    @pl.loop(1, GROUP)
    def _(i):
        to = lax.rem(me + (far_first(i) if axis == "member" else i), GROUP)
        pltpu.make_async_remote_copy(
            src.at[to], dst.at[me], send_sem, recv_sem, device_id={axis: to}, device_id_type=MESH
        ).start()

    pltpu.make_async_copy(src.at[me], dst.at[me], recv_sem).start()


def arrived(dst, recv_sem):
    pltpu.make_async_copy(dst, dst, recv_sem).wait()


def sent(src, send_sem):
    part = src.at[pl.ds(0, GROUP - 1)]
    pltpu.make_async_copy(part, part, send_sem).wait()


def partial_advance(qv, pm, wsend):
    for lev in range(LEV):
        x = qv[pm, lev]
        near = qv[pm, min(lev + 1, LEV - 1)] + qv[pm, max(lev - 1, 0)]
        side = lane_right(x, 1) + lane_left(x, 1)
        wsend[pm, lev, :, 0:NY] = 0.2 * ((near + side) + (strip_down(x) + strip_up(x))) - 0.2 * x
        for c in range(4):
            at = 128 * c
            wsend[pm, lev, c : c + 1, NY : NY + 128] = qv[pm, lev, 0:1, at : at + 128]
            wsend[pm, lev, c + 4 : c + 5, NY : NY + 128] = qv[pm, lev, CX - 1 : CX, at : at + 128]


def multigrid(pm, wrecv, perm, permt, work, fsend):
    plane = exact_dot(wrecv[pm, :, :, 0:NY].reshape(NX, NY), perm[...])
    for c in range(4):
        work[c] = plane[:, 128 * c : 128 * (c + 1)]
    edges = [wrecv[pm, :, c, NY : NY + 128] for c in range(8)]
    top = exact_dot(jnp.concatenate(edges[:4], axis=1), perm[...])
    bottom = exact_dot(jnp.concatenate(edges[4:], axis=1), perm[...])
    rows = []
    for rp in range(CX):
        x = [work[c, pl.ds(rp, GROUP, stride=CX), :] for c in range(4)]
        if rp == 0:
            x = [x[c] + 0.2 * strip_down(bottom[:, 128 * c : 128 * (c + 1)]) for c in range(4)]
        if rp == CX - 1:
            x = [x[c] + 0.2 * strip_up(top[:, 128 * c : 128 * (c + 1)]) for c in range(4)]
        rows.append(jnp.stack(x, axis=0))
    done = plane_forecast(rows)
    for rp in range(CX):
        for c in range(4):
            work[c, pl.ds(rp, GROUP, stride=CX), :] = done[rp][c]
    plane = jnp.concatenate([work[c] for c in range(4)], axis=1)
    fsend[pm] = exact_dot(plane, permt[...]).reshape(GROUP, CX, NY)


def column_means(pm, frecv, csend):
    total = frecv[pm, 0]
    for lev in range(1, LEV):
        total = total + frecv[pm, lev]
    total = total * (1.0 / LEV)
    for row in range(CX):
        for half in range(2):
            csend[2 * row + half, pm : pm + 1, :] = total[row : row + 1, half * HALF : (half + 1) * HALF]


def to_rows(pm, frecv, flat, zsend):
    for c in range(4):
        flat[c] = frecv[pm, :, :, 128 * c : 128 * (c + 1)].reshape(LEV * CX, 128)
    for row in range(CX):
        for c in range(4):
            at = 128 * (c % 2)
            zsend[pm, 2 * row + c // 2, :, at : at + 128] = flat[c, pl.ds(row, LEV, stride=CX), :]


def observation_sums(cols, vals, precs, masks, counts, row, half):
    first = pl.multiple_of(half * BLOCKS, BLOCKS)
    col = cols[row, pl.ds(first, BLOCKS), :]
    val = vals[row, pl.ds(first, BLOCKS), :]
    prec = precs[row, pl.ds(first, BLOCKS), :]
    mask = masks[row, pl.ds(first, BLOCKS), :].astype(f32)
    row_counts = counts[pl.ds(row, 1), :].astype(f32)
    lane = iota2((BLOCKS, 2 * BLOCKS), 1)
    mine = lane == iota2((BLOCKS, 2 * BLOCKS), 0) + half * BLOCKS
    count = jnp.sum(jnp.where(mine, jnp.broadcast_to(row_counts, mine.shape), 0.0), axis=1, keepdims=True)
    slot = iota2((BLOCKS, OBS), 1).astype(f32)
    weight = jnp.where(slot < count, mask * prec, 0.0)
    value = weight * val
    place = iota2((BLOCKS, HALF), 1)
    within = place & (BW - 1)
    wsum = jnp.zeros((BLOCKS, HALF), f32)
    vsum = jnp.zeros((BLOCKS, HALF), f32)
    for o in range(OBS):
        hit = within == col[:, o : o + 1]
        wsum = wsum + jnp.where(hit, weight[:, o : o + 1], 0.0)
        vsum = vsum + jnp.where(hit, value[:, o : o + 1], 0.0)
    own = (place >> 5) == iota2((BLOCKS, HALF), 0)
    return jnp.where(own, wsum, 0.0), jnp.where(own, vsum, 0.0)


def make_transform(crecv, wsum, vsum, cm, lhs, call, expand, emat):
    for m in range(GROUP):
        cm[64 + PER * m : 64 + PER * (m + 1), :] = crecv[m]
    means = cm[64 : 64 + ENS, :]
    pbar = jnp.mean(means, axis=0, keepdims=True)
    cm[0:64, :] = jnp.zeros((64, HALF), f32)
    cm[64 : 64 + ENS, :] = means - pbar
    cm[64 + ENS : 128, :] = jnp.zeros((16, HALF), f32)
    for j in range(ENS):
        lhs[8 * j : 8 * (j + 1), :] = wsum * cm[64 + j : 65 + j, :]
    lhs[8 * ENS : 8 * ENS + 8, :] = vsum - wsum * pbar
    system = lax.dot_general(
        lhs[...], cm[...], (((1,), (1,)), ((), ())), precision=lax.Precision.HIGHEST, preferred_element_type=f32
    )
    lane = iota2((BLOCKS, 128), 1)
    target = system[8 * ENS : 8 * ENS + 8, :]
    u = []
    for i in range(ENS):
        v = system[8 * i : 8 * (i + 1), :] + jnp.where(lane == i + 64, ENS - 1.0, jnp.where(lane == i, 1.0, 0.0))
        u.append(jnp.where(lane == 64 + ENS, target[:, 64 + i : 65 + i], v))
    weights = jnp.zeros((BLOCKS, 128), f32)
    wide = 8
    for first in range(0, ENS, wide):
        rows = u[first : first + wide]
        at = 64 + first
        pair = {
            (k, i): jnp.broadcast_to(rows[k][:, at + i : at + i + 1], (BLOCKS, 128))
            for k in range(wide)
            for i in range(k, wide)
        }
        low, inv, done = {}, [], []
        for k in range(wide):
            inv.append(1.0 / pair[k, k])
            for i in range(k + 1, wide):
                low[i, k] = pair[k, i] * inv[k]
            for m in range(k + 1, wide):
                for i in range(m, wide):
                    pair[m, i] = pair[m, i] - low[m, k] * pair[k, i]
        for k in range(wide):
            v = rows[k]
            for m in range(k):
                v = v - low[k, m] * done[m]
            done.append(v)
        back = [None] * wide
        for m in range(wide - 1, -1, -1):
            v = done[m] * inv[m]
            for k in range(m + 1, wide):
                v = v - low[k, m] * back[k]
            back[m] = v
        for i in range(first + wide, ENS):
            v = u[i]
            for k in range(wide):
                v = v - rows[k][:, 64 + i : 65 + i] * back[k]
            u[i] = v
        for k in range(wide):
            weights = weights + done[k] * (done[k][:, 64 + ENS : 65 + ENS] * inv[k])
            call[8 * (first + k) : 8 * (first + k) + 8, :] = done[k] * jnp.sqrt((ENS - 1.0) * inv[k])
    call[8 * ENS : 8 * ENS + 8, :] = weights
    call[8 * ENS + 8 :, :] = jnp.zeros((120, 128), f32)
    for g in range(4):
        count, depth = (16, 16 * (g + 1)) if g < 3 else (1, ENS)
        t = jnp.transpose(call[128 * g : 128 * (g + 1), :])[:depth]
        group = iota2((depth, 128), 1) >> 3
        high = t.astype(bf16).astype(f32)
        low = t - high
        parts = []
        for k in range(count):
            mine = group == k
            both = jnp.concatenate([jnp.where(mine, high, 0.0), jnp.where(mine, low, 0.0)], axis=1)
            parts.append(both.astype(bf16))
        wide = dot(jnp.concatenate(parts, axis=0), expand[...])
        for k in range(count):
            emat[16 * g + k, 0:depth, :] = wide[depth * k : depth * (k + 1), :]


def member_sum(zrecv, pm, total):
    for m in range(GROUP):
        total = zrecv[pm, m] if total is None else total + zrecv[pm, m]
    return total


def apply_transform(zrecv, total, emat, asend, arecv, send_sem, recv_sem):
    xbar = total * (1.0 / ENS)

    def mean_step(m, base):
        for pm in range(PER):
            x = zrecv[pm, m] - xbar
            zrecv[pm, m] = x
            base = base + x * emat[ENS, pl.ds(PER * m + pm, 1), :]
        return base

    base = lax.fori_loop(0, GROUP, mean_step, xbar)
    me = lax.axis_index("member")

    def one_target(to):
        def step(m, acc):
            acc = list(acc)
            for pm in range(PER):
                x = zrecv[pm, m]
                for n in range(PER):
                    acc[n] = acc[n] + x * emat[PER * to + n, pl.ds(PER * m + pm, 1), :]
            return tuple(acc)

        acc = lax.fori_loop(0, to, step, (base,) * PER)
        for n in range(PER):
            total = acc[n]
            for pm in range(n + 1):
                total = total + zrecv[pm, to] * emat[PER * to + n, pl.ds(PER * to + pm, 1), :]
            asend[to, n] = total

    @pl.loop(1, GROUP)
    def _(i):
        to = lax.rem(me + far_first(i), GROUP)
        one_target(to)
        pltpu.make_async_remote_copy(
            asend.at[to], arecv.at[me], send_sem, recv_sem, device_id={"member": to}, device_id_type=MESH
        ).start()

    one_target(me)
    pltpu.make_async_copy(asend.at[me], arecv.at[me], recv_sem).start()


def kernel(q, cols_in, vals_in, precs_in, masks_in, counts_in, arecv, qv, cols, vals, precs, masks, counts, wsend, wrecv,
           perm, permt, work, fsend, frecv, flat, zsend, zrecv, csend, crecv, cm, lhs, call, expand, emat, asend, lsem,
           ssem, rsem):
    given = ((q, qv), (cols_in, cols), (vals_in, vals), (precs_in, precs), (masks_in, masks), (counts_in, counts))
    loads = [pltpu.make_async_copy(a, b, lsem.at[n]) for n, (a, b) in enumerate(given)]
    for load in loads:
        load.start()
    barrier = pltpu.get_barrier_semaphore()
    for axis in ("member", "space"):
        me = lax.axis_index(axis)
        for i in (8, 7, 9, 6, 10, 5, 11, 4, 12, 3, 13, 2, 14, 1, 15):
            pl.semaphore_signal(barrier, inc=1, device_id={axis: lax.rem(me + i, GROUP)}, device_id_type=MESH)

    src = iota2((NY, NY), 0)
    dst = iota2((NY, NY), 1)
    perm[...] = (dst == ((src & 3) << 7) + (src >> 2)).astype(f32).astype(bf16)
    permt[...] = (src == ((dst & 3) << 7) + (dst >> 2)).astype(f32).astype(bf16)
    expand[...] = ((iota2((256, HALF), 0) & 7) == (iota2((256, HALF), 1) >> 5)).astype(f32).astype(bf16)
    loads[0].wait()
    for pm in range(PER):
        partial_advance(qv, pm, wsend)
    for load in loads[1:]:
        load.wait()
    member = lax.axis_index("member")
    wsum, vsum = observation_sums(cols, vals, precs, masks, counts, member // 2, lax.rem(member, 2))
    pl.semaphore_wait(barrier, 2 * (GROUP - 1))

    def to_planes(pm):
        send_all("space", wsend.at[pm], wrecv.at[pm], ssem.at[pm], rsem.at[pm])

    def solve(pm):
        arrived(wrecv.at[pm], rsem.at[pm])
        multigrid(pm, wrecv, perm, permt, work, fsend)
        send_all("space", fsend.at[pm], frecv.at[pm], ssem.at[3 + pm], rsem.at[3 + pm])

    def to_blocks(pm):
        arrived(frecv.at[pm], rsem.at[3 + pm])
        column_means(pm, frecv, csend)
        if pm == PER - 1:
            send_all("member", csend, crecv, ssem.at[9], rsem.at[9])
        to_rows(pm, frecv, flat, zsend)
        send_all("member", zsend.at[pm], zrecv.at[pm], ssem.at[6 + pm], rsem.at[6 + pm])

    to_planes(0)
    to_planes(1)
    solve(0)
    to_planes(2)
    solve(1)
    to_blocks(0)
    solve(2)
    to_blocks(1)
    to_blocks(2)
    arrived(zrecv.at[0], rsem.at[6])
    total = member_sum(zrecv, 0, None)
    arrived(crecv, rsem.at[9])
    make_transform(crecv, wsum, vsum, cm, lhs, call, expand, emat)
    arrived(zrecv.at[1], rsem.at[7])
    total = member_sum(zrecv, 1, total)
    arrived(zrecv.at[2], rsem.at[8])
    total = member_sum(zrecv, 2, total)
    apply_transform(zrecv, total, emat, asend, arecv, ssem.at[10], rsem.at[10])
    for pm in range(PER):
        sent(wsend.at[pm], ssem.at[pm])
        sent(fsend.at[pm], ssem.at[3 + pm])
        sent(zsend.at[pm], ssem.at[6 + pm])
    sent(csend, ssem.at[9])
    sent(asend, ssem.at[10])
    arrived(arecv, rsem.at[10])


def place(arecv, out, flat):
    for pm in range(PER):
        for m in range(GROUP):
            for c in range(2):
                at = 128 * c
                flat[pm, 2 * (m % 2) + c, pl.ds(m // 2, LEV, stride=CX), :] = arecv[m, pm, :, at : at + 128]
        for c in range(4):
            out[pm, :, 128 * c : 128 * (c + 1)] = flat[pm, c]


def local(q, cols, vals, precs, masks, counts):
    hbm = pl.BlockSpec(memory_space=pl.ANY)
    vmem = pl.BlockSpec(memory_space=pltpu.VMEM)
    strips = pltpu.VMEM((PER, LEV, CX, NY), f32)
    extended = pltpu.VMEM((PER, LEV, CX, NY + 128), f32)
    rows = pltpu.VMEM((PER, GROUP, LEV, HALF), f32)
    means = pltpu.VMEM((GROUP, PER, HALF), f32)
    slots = (CX, GROUP, OBS)
    dma = pltpu.SemaphoreType.DMA
    blocks = pl.pallas_call(
        kernel,
        out_shape=jax.ShapeDtypeStruct((GROUP, PER, LEV, HALF), f32),
        in_specs=[hbm] * 6,
        out_specs=hbm,
        scratch_shapes=[
            strips, pltpu.VMEM(slots, jnp.int32), pltpu.VMEM(slots, f32), pltpu.VMEM(slots, f32),
            pltpu.VMEM(slots, jnp.int32), pltpu.VMEM((CX, GROUP), jnp.int32), extended, extended,
            pltpu.VMEM((NY, NY), bf16), pltpu.VMEM((NY, NY), bf16), pltpu.VMEM((4, NX, 128), f32),
            strips, strips, pltpu.VMEM((4, LEV * CX, 128), f32), rows, rows, means, means,
            pltpu.VMEM((128, HALF), f32), pltpu.VMEM((8 * ENS + 8, HALF), f32), pltpu.VMEM((512, 128), f32),
            pltpu.VMEM((256, HALF), bf16), pltpu.VMEM((ENS + 1, ENS, HALF), f32),
            pltpu.VMEM((GROUP, PER, LEV, HALF), f32), dma((6,)), dma((11,)), dma((11,)),
        ],
        compiler_params=pltpu.CompilerParams(
            collective_id=0, has_side_effects=True, vmem_limit_bytes=56 * 1024 * 1024
        ),
        name="forecast_analysis",
    )(q, cols, vals, precs, masks, counts)
    out = pl.pallas_call(
        place,
        out_shape=jax.ShapeDtypeStruct((PER, LEV * CX, NY), f32),
        in_specs=[vmem],
        out_specs=vmem,
        scratch_shapes=[pltpu.VMEM((PER, 4, LEV * CX, 128), f32)],
        compiler_params=pltpu.CompilerParams(vmem_limit_bytes=56 * 1024 * 1024),
        name="place",
    )(blocks)
    return out.reshape(PER, LEV, CX, NY)


def solution(mesh):
    return jax.shard_map(
        local,
        mesh=mesh,
        in_specs=(
            P("member", None, "space", None),
            P("space", None, None),
            P("space", None, None),
            P("space", None, None),
            P("space", None, None),
            P("space", None),
        ),
        out_specs=P("member", None, "space", None),
        check_vma=False,
    )
```

```python
import functools
import math

import jax
import jax.numpy as jnp
from jax import lax
from jax.experimental import pallas as pl
from jax.experimental.pallas import tpu as pltpu
from jax.sharding import PartitionSpec as P

LEV, CX, BW, OBS, ENS, NX, NY = 16, 8, 32, 64, 48, 128, 512
GROUP = 16
PER = ENS // GROUP
HALF = NY // 2
BLOCKS = HALF // BW
SHIFT = 0.001
MESH = pl.DeviceIdType.MESH
f32, bf16 = jnp.float32, jnp.bfloat16


def split3(x):
    a = x.astype(bf16)
    r = x - a.astype(f32)
    b = r.astype(bf16)
    c = (r - b.astype(f32)).astype(bf16)
    return a, b, c


def dot(a, b):
    return jnp.dot(a, b, preferred_element_type=f32)


def exact_dot(x, selector):
    a, b, c = split3(x)
    return dot(a, selector) + (dot(b, selector) + dot(c, selector))


def iota2(shape, dim):
    return lax.broadcasted_iota(jnp.int32, shape, dim)


def lane_right(x, n):
    return jnp.where(iota2(x.shape, 1) < n, 0.0, pltpu.roll(x, n, 1))


def lane_left(x, n):
    return jnp.where(iota2(x.shape, 1) >= x.shape[1] - n, 0.0, pltpu.roll(x, x.shape[1] - n, 1))


def strip_down(x):
    return jnp.where(iota2(x.shape, 0) < 1, 0.0, pltpu.roll(x, 1, 0))


def strip_up(x):
    return jnp.where(iota2(x.shape, 0) >= x.shape[0] - 1, 0.0, pltpu.roll(x, x.shape[0] - 1, 0))


def each_phase(op, row):
    return jnp.stack([op(row[c]) for c in range(row.shape[0])], axis=0)


def neighbours(rows, width):
    count = len(rows)
    above = [each_phase(strip_down, rows[-1])] + rows[:-1]
    below = rows[1:] + [each_phase(strip_up, rows[0])]
    out = []
    for k in range(count):
        row = rows[k]
        phases = row.shape[0]
        first = lane_right(row[phases - 1], width)[None]
        last = lane_left(row[0], width)[None]
        if phases == 1:
            side = first + last
        else:
            side = jnp.concatenate([first, row[:-1]], axis=0) + jnp.concatenate([row[1:], last], axis=0)
        out.append((above[k] + below[k]) + side)
    return out


def smooth(p, f, level, width=1):
    h2 = 4.0**level
    d = SHIFT + 8.0 / h2
    a = 1.0 - (SHIFT + 4.0 / h2) / d
    n = neighbours(p, width)
    return [a * x + (1.0 / d) * y + (1.0 / (h2 * d)) * z for x, y, z in zip(p, f, n)]


def residual(p, f, level):
    h2 = 4.0**level
    n = neighbours(p, 1)
    return [y - (SHIFT + 4.0 / h2) * x + (1.0 / h2) * z for x, y, z in zip(p, f, n)]


def restrict(rows):
    out = []
    for k in range(len(rows) // 2):
        t = rows[2 * k] + rows[2 * k + 1]
        phases = t.shape[0]
        if phases == 1:
            even = (iota2(t[0].shape, 1) & 1) == 0
            other = jnp.where(even, pltpu.roll(t[0], 127, 1), pltpu.roll(t[0], 1, 1))
            out.append(0.25 * (t + other[None]))
        else:
            out.append(jnp.stack([0.25 * (t[2 * c] + t[2 * c + 1]) for c in range(phases // 2)], axis=0))
    return out


def add_prolonged(p, coarse):
    out = []
    for k in range(len(p)):
        c = coarse[k // 2]
        if c.shape[0] < p[k].shape[0]:
            c = jnp.stack([c[i // 2] for i in range(p[k].shape[0])], axis=0)
        out.append(p[k] + c)
    return out


def vcycle(p, f, level):
    d = SHIFT + 8.0 / 4.0**level
    if level == 3:
        p = [x * (1.0 / d) for x in f]
        for _ in range(2):
            p = smooth(p, f, 3, 2)
        return p
    if p is None:
        p = [x * (1.0 / d) for x in f]
    else:
        p = smooth(p, f, level)
    r = residual(p, f, level)
    c = vcycle(None, restrict(r), level + 1)
    p = add_prolonged(p, c)
    return smooth(p, f, level)


def plane_forecast(f):
    p = vcycle(None, f, 0)
    p = vcycle(p, f, 0)
    return [x - 0.04 * y for x, y in zip(f, p)]


def far_first(n):
    half = n // 2
    return GROUP // 2 + (2 * (n % 2) - 1) * half


def send_all(axis, src, dst, send_sem, recv_sem):
    me = lax.axis_index(axis)

    @pl.loop(1, GROUP)
    def _(i):
        to = lax.rem(me + (far_first(i) if axis == "member" else i), GROUP)
        pltpu.make_async_remote_copy(
            src.at[to], dst.at[me], send_sem, recv_sem, device_id={axis: to}, device_id_type=MESH
        ).start()

    pltpu.make_async_copy(src.at[me], dst.at[me], recv_sem).start()


def arrived(dst, recv_sem):
    pltpu.make_async_copy(dst, dst, recv_sem).wait()


def sent(src, send_sem):
    part = src.at[pl.ds(0, GROUP - 1)]
    pltpu.make_async_copy(part, part, send_sem).wait()


def partial_advance(qv, pm, wsend):
    for lev in range(LEV):
        x = qv[pm, lev]
        near = qv[pm, min(lev + 1, LEV - 1)] + qv[pm, max(lev - 1, 0)]
        side = lane_right(x, 1) + lane_left(x, 1)
        wsend[pm, lev, :, 0:NY] = 0.2 * ((near + side) + (strip_down(x) + strip_up(x))) - 0.2 * x
        for c in range(4):
            at = 128 * c
            wsend[pm, lev, c : c + 1, NY : NY + 128] = qv[pm, lev, 0:1, at : at + 128]
            wsend[pm, lev, c + 4 : c + 5, NY : NY + 128] = qv[pm, lev, CX - 1 : CX, at : at + 128]


def multigrid(pm, wrecv, perm, permt, work, fsend):
    plane = exact_dot(wrecv[pm, :, :, 0:NY].reshape(NX, NY), perm[...])
    for c in range(4):
        work[c] = plane[:, 128 * c : 128 * (c + 1)]
    edges = [wrecv[pm, :, c, NY : NY + 128] for c in range(8)]
    top = exact_dot(jnp.concatenate(edges[:4], axis=1), perm[...])
    bottom = exact_dot(jnp.concatenate(edges[4:], axis=1), perm[...])
    rows = []
    for rp in range(CX):
        x = [work[c, pl.ds(rp, GROUP, stride=CX), :] for c in range(4)]
        if rp == 0:
            x = [x[c] + 0.2 * strip_down(bottom[:, 128 * c : 128 * (c + 1)]) for c in range(4)]
        if rp == CX - 1:
            x = [x[c] + 0.2 * strip_up(top[:, 128 * c : 128 * (c + 1)]) for c in range(4)]
        rows.append(jnp.stack(x, axis=0))
    done = plane_forecast(rows)
    for rp in range(CX):
        for c in range(4):
            work[c, pl.ds(rp, GROUP, stride=CX), :] = done[rp][c]
    plane = jnp.concatenate([work[c] for c in range(4)], axis=1)
    fsend[pm] = exact_dot(plane, permt[...]).reshape(GROUP, CX, NY)


def column_means(pm, frecv, csend):
    total = frecv[pm, 0]
    for lev in range(1, LEV):
        total = total + frecv[pm, lev]
    total = total * (1.0 / LEV)
    for row in range(CX):
        for half in range(2):
            csend[2 * row + half, pm : pm + 1, :] = total[row : row + 1, half * HALF : (half + 1) * HALF]


def to_rows(given, flat, zsend):
    for c in range(4):
        flat[c] = given[:, :, 128 * c : 128 * (c + 1)].reshape(LEV * CX, 128)
    for row in range(CX):
        for c in range(4):
            zsend[c % 2, 2 * row + c // 2] = flat[c, pl.ds(row, LEV, stride=CX), :]


def observation_sums(cols, vals, precs, masks, counts, row, half):
    first = pl.multiple_of(half * BLOCKS, BLOCKS)
    col = cols[row, pl.ds(first, BLOCKS), :]
    val = vals[row, pl.ds(first, BLOCKS), :]
    prec = precs[row, pl.ds(first, BLOCKS), :]
    mask = masks[row, pl.ds(first, BLOCKS), :].astype(f32)
    row_counts = counts[pl.ds(row, 1), :].astype(f32)
    lane = iota2((BLOCKS, 2 * BLOCKS), 1)
    mine = lane == iota2((BLOCKS, 2 * BLOCKS), 0) + half * BLOCKS
    count = jnp.sum(jnp.where(mine, jnp.broadcast_to(row_counts, mine.shape), 0.0), axis=1, keepdims=True)
    slot = iota2((BLOCKS, OBS), 1).astype(f32)
    weight = jnp.where(slot < count, mask * prec, 0.0)
    value = weight * val
    place = iota2((BLOCKS, HALF), 1)
    within = place & (BW - 1)
    wsum = jnp.zeros((BLOCKS, HALF), f32)
    vsum = jnp.zeros((BLOCKS, HALF), f32)
    for o in range(OBS):
        hit = within == col[:, o : o + 1]
        wsum = wsum + jnp.where(hit, weight[:, o : o + 1], 0.0)
        vsum = vsum + jnp.where(hit, value[:, o : o + 1], 0.0)
    own = (place >> 5) == iota2((BLOCKS, HALF), 0)
    return jnp.where(own, wsum, 0.0), jnp.where(own, vsum, 0.0)


def make_transform(crecv, wsum, vsum, cm, lhs, call, expand, emat):
    for m in range(GROUP):
        cm[64 + PER * m : 64 + PER * (m + 1), :] = crecv[m]
    means = cm[64 : 64 + ENS, :]
    pbar = jnp.mean(means, axis=0, keepdims=True)
    cm[0:64, :] = jnp.zeros((64, HALF), f32)
    cm[64 : 64 + ENS, :] = means - pbar
    cm[64 + ENS : 128, :] = jnp.zeros((16, HALF), f32)
    for j in range(ENS):
        lhs[8 * j : 8 * (j + 1), :] = wsum * cm[64 + j : 65 + j, :]
    lhs[8 * ENS : 8 * ENS + 8, :] = vsum - wsum * pbar
    system = lax.dot_general(
        lhs[...], cm[...], (((1,), (1,)), ((), ())), precision=lax.Precision.HIGHEST, preferred_element_type=f32
    )
    lane = iota2((BLOCKS, 128), 1)
    target = system[8 * ENS : 8 * ENS + 8, :]
    u = []
    for i in range(ENS):
        v = system[8 * i : 8 * (i + 1), :] + jnp.where(lane == i + 64, ENS - 1.0, jnp.where(lane == i, 1.0, 0.0))
        u.append(jnp.where(lane == 64 + ENS, target[:, 64 + i : 65 + i], v))
    weights = jnp.zeros((BLOCKS, 128), f32)
    wide = 8
    for first in range(0, ENS, wide):
        rows = u[first : first + wide]
        at = 64 + first
        pair = {
            (k, i): jnp.broadcast_to(rows[k][:, at + i : at + i + 1], (BLOCKS, 128))
            for k in range(wide)
            for i in range(k, wide)
        }
        low, inv, done = {}, [], []
        for k in range(wide):
            inv.append(1.0 / pair[k, k])
            for i in range(k + 1, wide):
                low[i, k] = pair[k, i] * inv[k]
            for m in range(k + 1, wide):
                for i in range(m, wide):
                    pair[m, i] = pair[m, i] - low[m, k] * pair[k, i]
        for k in range(wide):
            v = rows[k]
            for m in range(k):
                v = v - low[k, m] * done[m]
            done.append(v)
        back = [None] * wide
        for m in range(wide - 1, -1, -1):
            v = done[m] * inv[m]
            for k in range(m + 1, wide):
                v = v - low[k, m] * back[k]
            back[m] = v
        for i in range(first + wide, ENS):
            v = u[i]
            for k in range(wide):
                v = v - rows[k][:, 64 + i : 65 + i] * back[k]
            u[i] = v
        for k in range(wide):
            weights = weights + done[k] * (done[k][:, 64 + ENS : 65 + ENS] * inv[k])
            call[8 * (first + k) : 8 * (first + k) + 8, :] = done[k] * jnp.sqrt((ENS - 1.0) * inv[k])
    call[8 * ENS : 8 * ENS + 8, :] = weights
    call[8 * ENS + 8 :, :] = jnp.zeros((120, 128), f32)
    for g in range(4):
        count, depth = (16, 16 * (g + 1)) if g < 3 else (1, ENS)
        t = jnp.transpose(call[128 * g : 128 * (g + 1), :])[:depth]
        group = iota2((depth, 128), 1) >> 3
        high = t.astype(bf16).astype(f32)
        low = t - high
        parts = []
        for k in range(count):
            mine = group == k
            both = jnp.concatenate([jnp.where(mine, high, 0.0), jnp.where(mine, low, 0.0)], axis=1)
            parts.append(both.astype(bf16))
        wide = dot(jnp.concatenate(parts, axis=0), expand[...])
        for k in range(count):
            for side in range(2):
                emat[side, 16 * g + k, 0:depth, :] = wide[depth * k : depth * (k + 1), 128 * side : 128 * (side + 1)]


def member_sum(part, total):
    for m in range(GROUP):
        total = part(m) if total is None else total + part(m)
    return total


def apply_transform(side, total, zrecv, emat, asend, arecv, send_sem, recv_sem):
    xbar = total * (1.0 / ENS)

    def member(pm, m):
        return zrecv[pm, side, m]

    def factor(k, j):
        return emat[side, k, pl.ds(j, 1), :]

    def mean_step(m, base):
        for pm in range(PER):
            x = member(pm, m) - xbar
            zrecv[pm, side, m] = x
            base = base + x * factor(ENS, PER * m + pm)
        return base

    base = lax.fori_loop(0, GROUP, mean_step, xbar)
    me = lax.axis_index("member")

    def one_target(to):
        def step(m, acc):
            acc = list(acc)
            for pm in range(PER):
                x = member(pm, m)
                for n in range(PER):
                    acc[n] = acc[n] + x * factor(PER * to + n, PER * m + pm)
            return tuple(acc)

        acc = lax.fori_loop(0, to, step, (base,) * PER)
        for n in range(PER):
            result = acc[n]
            for pm in range(n + 1):
                result = result + member(pm, to) * factor(PER * to + n, PER * to + pm)
            asend[side, to, n] = result

    @pl.loop(1, GROUP)
    def _(i):
        to = lax.rem(me + far_first(i), GROUP)
        one_target(to)
        pltpu.make_async_remote_copy(
            asend.at[side, to], arecv.at[side, me], send_sem, recv_sem, device_id={"member": to}, device_id_type=MESH
        ).start()

    one_target(me)
    pltpu.make_async_copy(asend.at[side, me], arecv.at[side, me], recv_sem).start()


def kernel(q, cols_in, vals_in, precs_in, masks_in, counts_in, arecv, qv, cols, vals, precs, masks, counts, wsend, wrecv,
           perm, permt, work, fsend, frecv, flat, zsend, zrecv, csend, crecv, cm, lhs, call, expand, emat, asend,
           lsem, ssem, rsem):
    given = ((q, qv), (cols_in, cols), (vals_in, vals), (precs_in, precs), (masks_in, masks), (counts_in, counts))
    loads = [pltpu.make_async_copy(a, b, lsem.at[n]) for n, (a, b) in enumerate(given)]
    for load in loads:
        load.start()
    barrier = pltpu.get_barrier_semaphore()
    for axis in ("member", "space"):
        me = lax.axis_index(axis)
        for i in (8, 7, 9, 6, 10, 5, 11, 4, 12, 3, 13, 2, 14, 1, 15):
            pl.semaphore_signal(barrier, inc=1, device_id={axis: lax.rem(me + i, GROUP)}, device_id_type=MESH)

    src = iota2((NY, NY), 0)
    dst = iota2((NY, NY), 1)
    perm[...] = (dst == ((src & 3) << 7) + (src >> 2)).astype(f32).astype(bf16)
    permt[...] = (src == ((dst & 3) << 7) + (dst >> 2)).astype(f32).astype(bf16)
    expand[...] = ((iota2((256, HALF), 0) & 7) == (iota2((256, HALF), 1) >> 5)).astype(f32).astype(bf16)
    loads[0].wait()
    for pm in range(PER):
        partial_advance(qv, pm, wsend)
    for load in loads[1:]:
        load.wait()
    member = lax.axis_index("member")
    wsum, vsum = observation_sums(cols, vals, precs, masks, counts, member // 2, lax.rem(member, 2))
    pl.semaphore_wait(barrier, 2 * (GROUP - 1))

    def to_planes(pm):
        send_all("space", wsend.at[pm], wrecv.at[pm], ssem.at[pm], rsem.at[pm])

    def solve(pm):
        arrived(wrecv.at[pm], rsem.at[pm])
        multigrid(pm, wrecv, perm, permt, work, fsend)
        send_all("space", fsend.at[pm], frecv.at[pm], ssem.at[3 + pm], rsem.at[3 + pm])

    def send_rows(pm, side):
        at = 6 + 2 * pm + side
        send_all("member", zsend.at[pm, side], zrecv.at[pm, side], ssem.at[at], rsem.at[at])

    def strips_back(pm):
        arrived(frecv.at[pm], rsem.at[3 + pm])
        to_rows(frecv.at[pm], flat, zsend.at[pm])

    for pm in range(PER):
        to_planes(pm)
    for pm in range(PER):
        solve(pm)
    strips_back(0)
    send_rows(0, 0)
    send_rows(0, 1)
    column_means(0, frecv, csend)
    strips_back(1)
    send_rows(1, 0)
    column_means(1, frecv, csend)
    strips_back(2)
    column_means(2, frecv, csend)
    send_all("member", csend, crecv, ssem.at[12], rsem.at[12])
    send_rows(2, 0)
    send_rows(1, 1)
    send_rows(2, 1)
    arrived(crecv, rsem.at[12])
    make_transform(crecv, wsum, vsum, cm, lhs, call, expand, emat)
    for side in range(2):
        total = None
        for pm in range(PER):
            arrived(zrecv.at[pm, side], rsem.at[6 + 2 * pm + side])
            total = member_sum(lambda m, pm=pm: zrecv[pm, side, m], total)
        apply_transform(side, total, zrecv, emat, asend, arecv, ssem.at[13 + side], rsem.at[13 + side])
    for pm in range(PER):
        sent(wsend.at[pm], ssem.at[pm])
        sent(fsend.at[pm], ssem.at[3 + pm])
    for side in range(2):
        for pm in range(PER):
            sent(zsend.at[pm, side], ssem.at[6 + 2 * pm + side])
    sent(csend, ssem.at[12])
    for side in range(2):
        sent(asend.at[side], ssem.at[13 + side])
        arrived(arecv.at[side], rsem.at[13 + side])


def place(arecv, out, flat):
    for pm in range(PER):
        for m in range(GROUP):
            for side in range(2):
                flat[pm, 2 * (m % 2) + side, pl.ds(m // 2, LEV, stride=CX), :] = arecv[side, m, pm]
        for c in range(4):
            out[pm, :, 128 * c : 128 * (c + 1)] = flat[pm, c]


def local(q, cols, vals, precs, masks, counts):
    hbm = pl.BlockSpec(memory_space=pl.ANY)
    vmem = pl.BlockSpec(memory_space=pltpu.VMEM)
    strips = pltpu.VMEM((PER, LEV, CX, NY), f32)
    extended = pltpu.VMEM((PER, LEV, CX, NY + 128), f32)
    halves = pltpu.VMEM((PER, 2, GROUP, LEV, 128), f32)
    means = pltpu.VMEM((GROUP, PER, HALF), f32)
    slots = (CX, GROUP, OBS)
    dma = pltpu.SemaphoreType.DMA
    blocks = pl.pallas_call(
        kernel,
        out_shape=jax.ShapeDtypeStruct((2, GROUP, PER, LEV, 128), f32),
        in_specs=[hbm] * 6,
        out_specs=hbm,
        scratch_shapes=[
            strips, pltpu.VMEM(slots, jnp.int32), pltpu.VMEM(slots, f32), pltpu.VMEM(slots, f32),
            pltpu.VMEM(slots, jnp.int32), pltpu.VMEM((CX, GROUP), jnp.int32), extended, extended,
            pltpu.VMEM((NY, NY), bf16), pltpu.VMEM((NY, NY), bf16), pltpu.VMEM((4, NX, 128), f32),
            strips, strips, pltpu.VMEM((4, LEV * CX, 128), f32), halves, halves, means, means,
            pltpu.VMEM((128, HALF), f32), pltpu.VMEM((8 * ENS + 8, HALF), f32), pltpu.VMEM((512, 128), f32),
            pltpu.VMEM((256, HALF), bf16), pltpu.VMEM((2, ENS + 1, ENS, 128), f32),
            pltpu.VMEM((2, GROUP, PER, LEV, 128), f32), dma((6,)), dma((15,)), dma((15,)),
        ],
        compiler_params=pltpu.CompilerParams(
            collective_id=0, has_side_effects=True, vmem_limit_bytes=56 * 1024 * 1024
        ),
        name="forecast_analysis",
    )(q, cols, vals, precs, masks, counts)
    out = pl.pallas_call(
        place,
        out_shape=jax.ShapeDtypeStruct((PER, LEV * CX, NY), f32),
        in_specs=[vmem],
        out_specs=vmem,
        scratch_shapes=[pltpu.VMEM((PER, 4, LEV * CX, 128), f32)],
        compiler_params=pltpu.CompilerParams(vmem_limit_bytes=56 * 1024 * 1024),
        name="place",
    )(blocks)
    return out.reshape(PER, LEV, CX, NY)


def solution(mesh):
    return jax.shard_map(
        local,
        mesh=mesh,
        in_specs=(
            P("member", None, "space", None),
            P("space", None, None),
            P("space", None, None),
            P("space", None, None),
            P("space", None, None),
            P("space", None),
        ),
        out_specs=P("member", None, "space", None),
        check_vma=False,
    )
```

```python
import functools
import math

import jax
import jax.numpy as jnp
from jax import lax
from jax.experimental import pallas as pl
from jax.experimental.pallas import tpu as pltpu
from jax.sharding import PartitionSpec as P

LEV, CX, BW, OBS, ENS, NX, NY = 16, 8, 32, 64, 48, 128, 512
GROUP = 16
PER = ENS // GROUP
HALF = NY // 2
BLOCKS = HALF // BW
SHIFT = 0.001
MESH = pl.DeviceIdType.MESH
f32, bf16 = jnp.float32, jnp.bfloat16


def split3(x):
    a = x.astype(bf16)
    r = x - a.astype(f32)
    b = r.astype(bf16)
    c = (r - b.astype(f32)).astype(bf16)
    return a, b, c


def dot(a, b):
    return jnp.dot(a, b, preferred_element_type=f32)


def exact_dot(x, selector):
    a, b, c = split3(x)
    return dot(a, selector) + (dot(b, selector) + dot(c, selector))


def iota2(shape, dim):
    return lax.broadcasted_iota(jnp.int32, shape, dim)


def lane_right(x, n):
    return jnp.where(iota2(x.shape, 1) < n, 0.0, pltpu.roll(x, n, 1))


def lane_left(x, n):
    return jnp.where(iota2(x.shape, 1) >= x.shape[1] - n, 0.0, pltpu.roll(x, x.shape[1] - n, 1))


def strip_down(x):
    return jnp.where(iota2(x.shape, 0) < 1, 0.0, pltpu.roll(x, 1, 0))


def strip_up(x):
    return jnp.where(iota2(x.shape, 0) >= x.shape[0] - 1, 0.0, pltpu.roll(x, x.shape[0] - 1, 0))


def each_phase(op, row):
    return jnp.stack([op(row[c]) for c in range(row.shape[0])], axis=0)


def neighbours(rows, width):
    count = len(rows)
    above = [each_phase(strip_down, rows[-1])] + rows[:-1]
    below = rows[1:] + [each_phase(strip_up, rows[0])]
    out = []
    for k in range(count):
        row = rows[k]
        phases = row.shape[0]
        first = lane_right(row[phases - 1], width)[None]
        last = lane_left(row[0], width)[None]
        if phases == 1:
            side = first + last
        else:
            side = jnp.concatenate([first, row[:-1]], axis=0) + jnp.concatenate([row[1:], last], axis=0)
        out.append((above[k] + below[k]) + side)
    return out


def smooth(p, f, level, width=1):
    h2 = 4.0**level
    d = SHIFT + 8.0 / h2
    a = 1.0 - (SHIFT + 4.0 / h2) / d
    n = neighbours(p, width)
    return [a * x + (1.0 / d) * y + (1.0 / (h2 * d)) * z for x, y, z in zip(p, f, n)]


def residual(p, f, level):
    h2 = 4.0**level
    n = neighbours(p, 1)
    return [y - (SHIFT + 4.0 / h2) * x + (1.0 / h2) * z for x, y, z in zip(p, f, n)]


def restrict(rows):
    out = []
    for k in range(len(rows) // 2):
        t = rows[2 * k] + rows[2 * k + 1]
        phases = t.shape[0]
        if phases == 1:
            even = (iota2(t[0].shape, 1) & 1) == 0
            other = jnp.where(even, pltpu.roll(t[0], 127, 1), pltpu.roll(t[0], 1, 1))
            out.append(0.25 * (t + other[None]))
        else:
            out.append(jnp.stack([0.25 * (t[2 * c] + t[2 * c + 1]) for c in range(phases // 2)], axis=0))
    return out


def add_prolonged(p, coarse):
    out = []
    for k in range(len(p)):
        c = coarse[k // 2]
        if c.shape[0] < p[k].shape[0]:
            c = jnp.stack([c[i // 2] for i in range(p[k].shape[0])], axis=0)
        out.append(p[k] + c)
    return out


def vcycle(p, f, level):
    d = SHIFT + 8.0 / 4.0**level
    if level == 3:
        p = [x * (1.0 / d) for x in f]
        for _ in range(2):
            p = smooth(p, f, 3, 2)
        return p
    if p is None:
        p = [x * (1.0 / d) for x in f]
    else:
        p = smooth(p, f, level)
    r = residual(p, f, level)
    c = vcycle(None, restrict(r), level + 1)
    p = add_prolonged(p, c)
    return smooth(p, f, level)


def plane_forecast(f):
    p = vcycle(None, f, 0)
    p = vcycle(p, f, 0)
    return [x - 0.04 * y for x, y in zip(f, p)]


def far_first(n):
    half = n // 2
    return GROUP // 2 + (2 * (n % 2) - 1) * half


def send_all(axis, src, dst, send_sem, recv_sem):
    me = lax.axis_index(axis)

    @pl.loop(1, GROUP)
    def _(i):
        to = lax.rem(me + (far_first(i) if axis == "member" else i), GROUP)
        pltpu.make_async_remote_copy(
            src.at[to], dst.at[me], send_sem, recv_sem, device_id={axis: to}, device_id_type=MESH
        ).start()

    pltpu.make_async_copy(src.at[me], dst.at[me], recv_sem).start()


def arrived(dst, recv_sem):
    pltpu.make_async_copy(dst, dst, recv_sem).wait()


def sent(src, send_sem):
    part = src.at[pl.ds(0, GROUP - 1)]
    pltpu.make_async_copy(part, part, send_sem).wait()


def partial_advance(qv, pm, wsend):
    for lev in range(LEV):
        x = qv[pm, lev]
        near = qv[pm, min(lev + 1, LEV - 1)] + qv[pm, max(lev - 1, 0)]
        side = lane_right(x, 1) + lane_left(x, 1)
        wsend[pm, lev, :, 0:NY] = 0.2 * ((near + side) + (strip_down(x) + strip_up(x))) - 0.2 * x
        for c in range(4):
            at = 128 * c
            wsend[pm, lev, c : c + 1, NY : NY + 128] = qv[pm, lev, 0:1, at : at + 128]
            wsend[pm, lev, c + 4 : c + 5, NY : NY + 128] = qv[pm, lev, CX - 1 : CX, at : at + 128]


def multigrid(pm, wrecv, perm, permt, work, fsend):
    plane = exact_dot(wrecv[pm, :, :, 0:NY].reshape(NX, NY), perm[...])
    for c in range(4):
        work[c] = plane[:, 128 * c : 128 * (c + 1)]
    edges = [wrecv[pm, :, c, NY : NY + 128] for c in range(8)]
    top = exact_dot(jnp.concatenate(edges[:4], axis=1), perm[...])
    bottom = exact_dot(jnp.concatenate(edges[4:], axis=1), perm[...])
    rows = []
    for rp in range(CX):
        x = [work[c, pl.ds(rp, GROUP, stride=CX), :] for c in range(4)]
        if rp == 0:
            x = [x[c] + 0.2 * strip_down(bottom[:, 128 * c : 128 * (c + 1)]) for c in range(4)]
        if rp == CX - 1:
            x = [x[c] + 0.2 * strip_up(top[:, 128 * c : 128 * (c + 1)]) for c in range(4)]
        rows.append(jnp.stack(x, axis=0))
    done = plane_forecast(rows)
    for rp in range(CX):
        for c in range(4):
            work[c, pl.ds(rp, GROUP, stride=CX), :] = done[rp][c]
    plane = jnp.concatenate([work[c] for c in range(4)], axis=1)
    fsend[pm] = exact_dot(plane, permt[...]).reshape(GROUP, CX, NY)


def column_means(pm, frecv, csend):
    total = frecv[pm, 0]
    for lev in range(1, LEV):
        total = total + frecv[pm, lev]
    total = total * (1.0 / LEV)
    for row in range(CX):
        for half in range(2):
            csend[2 * row + half, pm : pm + 1, :] = total[row : row + 1, half * HALF : (half + 1) * HALF]


def to_rows(given, flat, zsend):
    for c in range(4):
        flat[c] = given[:, :, 128 * c : 128 * (c + 1)].reshape(LEV * CX, 128)
    for row in range(CX):
        for c in range(4):
            zsend[c % 2, 2 * row + c // 2] = flat[c, pl.ds(row, LEV, stride=CX), :]


def observation_sums(cols, vals, precs, masks, counts, row, half):
    first = pl.multiple_of(half * BLOCKS, BLOCKS)
    col = cols[row, pl.ds(first, BLOCKS), :]
    val = vals[row, pl.ds(first, BLOCKS), :]
    prec = precs[row, pl.ds(first, BLOCKS), :]
    mask = masks[row, pl.ds(first, BLOCKS), :].astype(f32)
    row_counts = counts[pl.ds(row, 1), :].astype(f32)
    lane = iota2((BLOCKS, 2 * BLOCKS), 1)
    mine = lane == iota2((BLOCKS, 2 * BLOCKS), 0) + half * BLOCKS
    count = jnp.sum(jnp.where(mine, jnp.broadcast_to(row_counts, mine.shape), 0.0), axis=1, keepdims=True)
    slot = iota2((BLOCKS, OBS), 1).astype(f32)
    weight = jnp.where(slot < count, mask * prec, 0.0)
    value = weight * val
    place = iota2((BLOCKS, HALF), 1)
    within = place & (BW - 1)
    wsum = jnp.zeros((BLOCKS, HALF), f32)
    vsum = jnp.zeros((BLOCKS, HALF), f32)
    for o in range(OBS):
        hit = within == col[:, o : o + 1]
        wsum = wsum + jnp.where(hit, weight[:, o : o + 1], 0.0)
        vsum = vsum + jnp.where(hit, value[:, o : o + 1], 0.0)
    own = (place >> 5) == iota2((BLOCKS, HALF), 0)
    return jnp.where(own, wsum, 0.0), jnp.where(own, vsum, 0.0)


def make_transform(crecv, wsum, vsum, cm, lhs, call, expand, emat):
    for m in range(GROUP):
        cm[64 + PER * m : 64 + PER * (m + 1), :] = crecv[m]
    means = cm[64 : 64 + ENS, :]
    pbar = jnp.mean(means, axis=0, keepdims=True)
    cm[0:64, :] = jnp.zeros((64, HALF), f32)
    cm[64 : 64 + ENS, :] = means - pbar
    cm[64 + ENS : 128, :] = jnp.zeros((16, HALF), f32)
    for j in range(ENS):
        lhs[8 * j : 8 * (j + 1), :] = wsum * cm[64 + j : 65 + j, :]
    lhs[8 * ENS : 8 * ENS + 8, :] = vsum - wsum * pbar
    system = lax.dot_general(
        lhs[...], cm[...], (((1,), (1,)), ((), ())), precision=lax.Precision.HIGHEST, preferred_element_type=f32
    )
    lane = iota2((BLOCKS, 128), 1)
    target = system[8 * ENS : 8 * ENS + 8, :]
    u = []
    for i in range(ENS):
        v = system[8 * i : 8 * (i + 1), :] + jnp.where(lane == i + 64, ENS - 1.0, jnp.where(lane == i, 1.0, 0.0))
        u.append(jnp.where(lane == 64 + ENS, target[:, 64 + i : 65 + i], v))
    weights = jnp.zeros((BLOCKS, 128), f32)
    wide = 8
    for first in range(0, ENS, wide):
        rows = u[first : first + wide]
        at = 64 + first
        pair = {
            (k, i): jnp.broadcast_to(rows[k][:, at + i : at + i + 1], (BLOCKS, 128))
            for k in range(wide)
            for i in range(k, wide)
        }
        low, inv, done = {}, [], []
        for k in range(wide):
            inv.append(1.0 / pair[k, k])
            for i in range(k + 1, wide):
                low[i, k] = pair[k, i] * inv[k]
            for m in range(k + 1, wide):
                for i in range(m, wide):
                    pair[m, i] = pair[m, i] - low[m, k] * pair[k, i]
        for k in range(wide):
            v = rows[k]
            for m in range(k):
                v = v - low[k, m] * done[m]
            done.append(v)
        back = [None] * wide
        for m in range(wide - 1, -1, -1):
            v = done[m] * inv[m]
            for k in range(m + 1, wide):
                v = v - low[k, m] * back[k]
            back[m] = v
        for i in range(first + wide, ENS):
            v = u[i]
            for k in range(wide):
                v = v - rows[k][:, 64 + i : 65 + i] * back[k]
            u[i] = v
        for k in range(wide):
            weights = weights + done[k] * (done[k][:, 64 + ENS : 65 + ENS] * inv[k])
            call[8 * (first + k) : 8 * (first + k) + 8, :] = done[k] * jnp.sqrt((ENS - 1.0) * inv[k])
    call[8 * ENS : 8 * ENS + 8, :] = weights
    call[8 * ENS + 8 :, :] = jnp.zeros((120, 128), f32)
    for g in range(4):
        count, depth = (16, 16 * (g + 1)) if g < 3 else (1, ENS)
        t = jnp.transpose(call[128 * g : 128 * (g + 1), :])[:depth]
        group = iota2((depth, 128), 1) >> 3
        high = t.astype(bf16).astype(f32)
        low = t - high
        parts = []
        for k in range(count):
            mine = group == k
            both = jnp.concatenate([jnp.where(mine, high, 0.0), jnp.where(mine, low, 0.0)], axis=1)
            parts.append(both.astype(bf16))
        wide = dot(jnp.concatenate(parts, axis=0), expand[...])
        for k in range(count):
            for side in range(2):
                emat[side, 16 * g + k, 0:depth, :] = wide[depth * k : depth * (k + 1), 128 * side : 128 * (side + 1)]


def member_sum(part, total):
    for m in range(GROUP):
        total = part(m) if total is None else total + part(m)
    return total


def apply_transform(side, total, zrecv, emat, asend, arecv, send_sem, recv_sem):
    xbar = total * (1.0 / ENS)

    def member(pm, m):
        return zrecv[pm, side, m]

    def factor(k, j):
        return emat[side, k, pl.ds(j, 1), :]

    def mean_step(m, base):
        for pm in range(PER):
            x = member(pm, m) - xbar
            zrecv[pm, side, m] = x
            base = base + x * factor(ENS, PER * m + pm)
        return base

    base = lax.fori_loop(0, GROUP, mean_step, xbar)
    me = lax.axis_index("member")

    def one_target(to):
        def step(m, acc):
            acc = list(acc)
            for pm in range(PER):
                x = member(pm, m)
                for n in range(PER):
                    acc[n] = acc[n] + x * factor(PER * to + n, PER * m + pm)
            return tuple(acc)

        acc = lax.fori_loop(0, to, step, (base,) * PER)
        for n in range(PER):
            result = acc[n]
            for pm in range(n + 1):
                result = result + member(pm, to) * factor(PER * to + n, PER * to + pm)
            asend[side, to, n] = result

    @pl.loop(1, GROUP)
    def _(i):
        to = lax.rem(me + far_first(i), GROUP)
        one_target(to)
        pltpu.make_async_remote_copy(
            asend.at[side, to], arecv.at[side, me], send_sem, recv_sem, device_id={"member": to}, device_id_type=MESH
        ).start()

    one_target(me)
    pltpu.make_async_copy(asend.at[side, me], arecv.at[side, me], recv_sem).start()


def kernel(q, cols_in, vals_in, precs_in, masks_in, counts_in, arecv, qv, cols, vals, precs, masks, counts, wsend, wrecv,
           perm, permt, work, fsend, frecv, flat, zsend, zrecv, csend, crecv, cm, lhs, call, expand, emat, asend,
           lsem, ssem, rsem):
    given = ((q, qv), (cols_in, cols), (vals_in, vals), (precs_in, precs), (masks_in, masks), (counts_in, counts))
    loads = [pltpu.make_async_copy(a, b, lsem.at[n]) for n, (a, b) in enumerate(given)]
    for load in loads:
        load.start()
    barrier = pltpu.get_barrier_semaphore()
    for axis in ("member", "space"):
        me = lax.axis_index(axis)
        for i in (8, 7, 9, 6, 10, 5, 11, 4, 12, 3, 13, 2, 14, 1, 15):
            pl.semaphore_signal(barrier, inc=1, device_id={axis: lax.rem(me + i, GROUP)}, device_id_type=MESH)

    loads[0].wait()
    partial_advance(qv, 0, wsend)
    pl.semaphore_wait(barrier, 2 * (GROUP - 1))

    def to_planes(pm):
        send_all("space", wsend.at[pm], wrecv.at[pm], ssem.at[pm], rsem.at[pm])

    to_planes(0)
    for pm in range(1, PER):
        partial_advance(qv, pm, wsend)
        to_planes(pm)
    src = iota2((NY, NY), 0)
    dst = iota2((NY, NY), 1)
    perm[...] = (dst == ((src & 3) << 7) + (src >> 2)).astype(f32).astype(bf16)
    permt[...] = (src == ((dst & 3) << 7) + (dst >> 2)).astype(f32).astype(bf16)
    expand[...] = ((iota2((256, HALF), 0) & 7) == (iota2((256, HALF), 1) >> 5)).astype(f32).astype(bf16)
    for load in loads[1:]:
        load.wait()
    member = lax.axis_index("member")
    wsum, vsum = observation_sums(cols, vals, precs, masks, counts, member // 2, lax.rem(member, 2))

    def solve(pm):
        arrived(wrecv.at[pm], rsem.at[pm])
        multigrid(pm, wrecv, perm, permt, work, fsend)
        send_all("space", fsend.at[pm], frecv.at[pm], ssem.at[3 + pm], rsem.at[3 + pm])

    def send_rows(pm, side):
        at = 6 + 2 * pm + side
        send_all("member", zsend.at[pm, side], zrecv.at[pm, side], ssem.at[at], rsem.at[at])

    def strips_back(pm):
        arrived(frecv.at[pm], rsem.at[3 + pm])
        to_rows(frecv.at[pm], flat, zsend.at[pm])

    for pm in range(PER):
        solve(pm)
    strips_back(0)
    send_rows(0, 0)
    send_rows(0, 1)
    column_means(0, frecv, csend)
    strips_back(1)
    column_means(1, frecv, csend)
    strips_back(2)
    column_means(2, frecv, csend)
    send_all("member", csend, crecv, ssem.at[12], rsem.at[12])
    send_rows(1, 0)
    send_rows(2, 0)
    send_rows(1, 1)
    send_rows(2, 1)
    arrived(crecv, rsem.at[12])
    make_transform(crecv, wsum, vsum, cm, lhs, call, expand, emat)
    for side in range(2):
        total = None
        for pm in range(PER):
            arrived(zrecv.at[pm, side], rsem.at[6 + 2 * pm + side])
            total = member_sum(lambda m, pm=pm: zrecv[pm, side, m], total)
        apply_transform(side, total, zrecv, emat, asend, arecv, ssem.at[13 + side], rsem.at[13 + side])
    for pm in range(PER):
        sent(wsend.at[pm], ssem.at[pm])
        sent(fsend.at[pm], ssem.at[3 + pm])
    for side in range(2):
        for pm in range(PER):
            sent(zsend.at[pm, side], ssem.at[6 + 2 * pm + side])
    sent(csend, ssem.at[12])
    for side in range(2):
        sent(asend.at[side], ssem.at[13 + side])
        arrived(arecv.at[side], rsem.at[13 + side])


def place(arecv, out, flat):
    for pm in range(PER):
        for m in range(GROUP):
            for side in range(2):
                flat[pm, 2 * (m % 2) + side, pl.ds(m // 2, LEV, stride=CX), :] = arecv[side, m, pm]
        for c in range(4):
            out[pm, :, 128 * c : 128 * (c + 1)] = flat[pm, c]


def local(q, cols, vals, precs, masks, counts):
    hbm = pl.BlockSpec(memory_space=pl.ANY)
    vmem = pl.BlockSpec(memory_space=pltpu.VMEM)
    strips = pltpu.VMEM((PER, LEV, CX, NY), f32)
    extended = pltpu.VMEM((PER, LEV, CX, NY + 128), f32)
    halves = pltpu.VMEM((PER, 2, GROUP, LEV, 128), f32)
    means = pltpu.VMEM((GROUP, PER, HALF), f32)
    slots = (CX, GROUP, OBS)
    dma = pltpu.SemaphoreType.DMA
    blocks = pl.pallas_call(
        kernel,
        out_shape=jax.ShapeDtypeStruct((2, GROUP, PER, LEV, 128), f32),
        in_specs=[hbm] * 6,
        out_specs=hbm,
        scratch_shapes=[
            strips, pltpu.VMEM(slots, jnp.int32), pltpu.VMEM(slots, f32), pltpu.VMEM(slots, f32),
            pltpu.VMEM(slots, jnp.int32), pltpu.VMEM((CX, GROUP), jnp.int32), extended, extended,
            pltpu.VMEM((NY, NY), bf16), pltpu.VMEM((NY, NY), bf16), pltpu.VMEM((4, NX, 128), f32),
            strips, strips, pltpu.VMEM((4, LEV * CX, 128), f32), halves, halves, means, means,
            pltpu.VMEM((128, HALF), f32), pltpu.VMEM((8 * ENS + 8, HALF), f32), pltpu.VMEM((512, 128), f32),
            pltpu.VMEM((256, HALF), bf16), pltpu.VMEM((2, ENS + 1, ENS, 128), f32),
            pltpu.VMEM((2, GROUP, PER, LEV, 128), f32), dma((6,)), dma((15,)), dma((15,)),
        ],
        compiler_params=pltpu.CompilerParams(
            collective_id=0, has_side_effects=True, vmem_limit_bytes=56 * 1024 * 1024
        ),
        name="forecast_analysis",
    )(q, cols, vals, precs, masks, counts)
    out = pl.pallas_call(
        place,
        out_shape=jax.ShapeDtypeStruct((PER, LEV * CX, NY), f32),
        in_specs=[vmem],
        out_specs=vmem,
        scratch_shapes=[pltpu.VMEM((PER, 4, LEV * CX, 128), f32)],
        compiler_params=pltpu.CompilerParams(vmem_limit_bytes=56 * 1024 * 1024),
        name="place",
    )(blocks)
    return out.reshape(PER, LEV, CX, NY)


def solution(mesh):
    return jax.shard_map(
        local,
        mesh=mesh,
        in_specs=(
            P("member", None, "space", None),
            P("space", None, None),
            P("space", None, None),
            P("space", None, None),
            P("space", None, None),
            P("space", None),
        ),
        out_specs=P("member", None, "space", None),
        check_vma=False,
    )
```
